256 devices in a mesh: seq: 32 (over x_hi, z, core), head: 8 (over y, x_lo).
Axes of the slice: x: 4 (x_hi: 2, x_lo: 2; x = x_hi * 2 + x_lo), y: 4, z: 8, core: 2. Of those that a mesh axis runs over, the one named last changes fastest.
Arguments:
- queries: bfloat16 [8192, 8192], P(('seq', 'head')), may hold values from -6 to 6
- keys: bfloat16 [8192, 1024], P(('seq', 'head')), may hold values from -6 to 6
- values: bfloat16 [8192, 1024], P(('seq', 'head')), may hold values from -6 to 6
- grad_out: bfloat16 [8192, 8192], P(('seq', 'head')), may hold values from -6 to 6
- doc_blocks: int32 [16], replicated, may hold values from 1 to 8, 64 in all
Outputs:
- attended: bfloat16 [8192, 8192], P('seq', 'head')
- grad_queries: bfloat16 [8192, 8192], P('seq', 'head')
- grad_keys: bfloat16 [8192, 1024], P('seq', 'head')
- grad_values: bfloat16 [8192, 1024], P('seq', 'head')
The draws below stay inside these ranges and needn't reach their ends.
Inputs may be any that keep to these rules, and one draw needn't show every extreme that they name: `doc_blocks`: the lengths sum to 64; the largest is exactly 8 blocks in every draw.
All inputs are finite; a program needn't handle non-finite values.
Results may differ from the reference program's by a relative error of at most 0.029.
Values may be sent and summed in bfloat16 or wider, within the bound.
No kernel may reach another device: no remote copies, remote signals or barrier semaphores. Data moves between devices by JAX's collectives and lax.ppermute only.
A program may use at most 64 MiB of HBM per device.

```python
import math
import jax
import jax.numpy as jnp
import numpy as np
from jax import lax

HD = 128
QH_DEV = 8
TOK_DEV = 256
SPAN = 4
KVH = 8
QH = 64
TOKENS = 8192
NDOCS = 16
N_SEQ = 32
N_HEAD = 8


def draw_queries(key, part):
    base = jnp.clip(jax.random.normal(jax.random.fold_in(key, 1), (TOKENS, QH * HD), jnp.float32), -5.5, 5.5)
    return base.astype(jnp.bfloat16)


def draw_keys(key, part):
    base = jnp.clip(jax.random.normal(jax.random.fold_in(key, 2), (TOKENS, KVH * HD), jnp.float32), -5.5, 5.5)
    return base.astype(jnp.bfloat16)


def level_of(stream_key, shape, cuts, least, high):
    level, own = 1.0, jax.random.fold_in(stream_key, 6)
    for position, shards_of in cuts:
        draws = jnp.exp(jax.random.uniform(jax.random.fold_in(own, position), (shards_of,), jnp.float32, least / len(cuts), high / len(cuts)))
        level = level * jnp.repeat(draws, shape[position] // shards_of).reshape([-1 if axis == position else 1 for axis in range(len(shape))])
    return level


def profile(number_of, total, limit, skew):
    portions = [(1 << 20) // math.isqrt(grade ** skew) + 1 for grade in range(2, number_of + 1)]
    surplus, counts = total - limit - (number_of - 1), [1] * (number_of - 1)
    while surplus > 0:
        movable = [i for i in range(number_of - 1) if counts[i] < limit]
        pool, left = sum([portions[i] for i in movable]), surplus
        for i in movable:
            extra = min(limit - counts[i], max(1, left * portions[i] // pool), surplus)
            counts[i] = counts[i] + extra
            surplus = surplus - extra
    return np.array([limit] + counts)


def uneven(stream_key, count, total, limit, skew):
    if count == 2:
        one = jax.random.randint(stream_key, (), max(1, total - limit), min(limit, total - 1) + 1)
        return jnp.stack([one, total - one])
    sizes = jnp.asarray(profile(count, total, limit, skew), jnp.int32)
    twos = (count - 1) // 2
    source_of, sink = sizes[1:1 + 2 * twos:2], sizes[2:2 + 2 * twos:2]
    margin = jnp.minimum(source_of - 1, limit - sink)
    shifted = jax.random.randint(jax.random.fold_in(stream_key, 1), (twos,), 0, 1 << 20) % (margin + 1)
    sizes = sizes.at[1:1 + 2 * twos:2].set(source_of - shifted).at[2:2 + 2 * twos:2].set(sink + shifted)
    return sizes[jax.random.permutation(jax.random.fold_in(stream_key, 2), count)]


def gaussian(own_key, dims, scale, most, cuts=(), kind=jnp.bfloat16):
    result = jax.random.normal(own_key, dims, jnp.float32) * scale
    if len(cuts) > 0:
        result = level_of(own_key, dims, cuts, -0.22, 0.18) * result
    return jnp.clip(result, min=-most, max=most).astype(kind)


def setup_inputs(seed: int = 0) -> dict:
    arg_keys = jax.random.split(jax.random.key(seed), 6)
    queries = draw_queries(jax.random.fold_in(arg_keys[5], 71), 0)
    keys = draw_keys(jax.random.fold_in(arg_keys[5], 71), 0)
    values = gaussian(arg_keys[2], (TOKENS, KVH * HD), 1.0, 6.0, ((0, 256),))
    grad_out = gaussian(arg_keys[3], (TOKENS, QH * HD), 1.0, 6.0, ((0, 256),))
    doc_blocks = uneven(arg_keys[4], NDOCS, TOKENS // 128, SPAN * TOK_DEV // 128, 2).astype(jnp.int32)
    return {"queries": queries, "keys": keys, "values": values, "grad_out": grad_out, "doc_blocks": doc_blocks}


def segment_of(positions, block_ends):
    counted = jnp.sum((positions[:, None] >= block_ends[None, :]).astype(jnp.int32), axis=1)
    return jnp.where(positions < 0, -1, counted)


def attend(query_rows, key_rows, value_rows, grad_rows, allowed, scale):
    high = lax.Precision.HIGHEST
    query_full = query_rows.astype(jnp.float32)
    key_full = key_rows.astype(jnp.float32)
    value_full = value_rows.astype(jnp.float32)
    grad_full = grad_rows.astype(jnp.float32)
    scores = jnp.einsum("rhd,wd->hrw", query_full, key_full, precision=high) * scale
    scores = jnp.where(allowed[None], scores, -1e30)
    highest = jnp.max(scores, axis=2, keepdims=True)
    weights = jnp.exp(scores - highest)
    probs = weights / jnp.sum(weights, axis=2, keepdims=True)
    probs_low = probs.astype(jnp.bfloat16)
    attended = jnp.einsum("hrw,wd->rhd", probs_low.astype(jnp.float32), value_full, precision=high).astype(jnp.bfloat16)
    grad_probs = jnp.einsum("rhd,wd->hrw", grad_full, value_full, precision=high)
    delta = jnp.sum(grad_full * attended.astype(jnp.float32), axis=2)
    grad_scores = (probs * (grad_probs - jnp.transpose(delta)[:, :, None])).astype(jnp.bfloat16)
    grad_low = grad_scores.astype(jnp.float32)
    grad_query = (jnp.einsum("hrw,wd->rhd", grad_low, key_full, precision=high) * scale).astype(jnp.bfloat16)
    grad_key = jnp.einsum("hrw,rhd->wd", grad_low, query_full, precision=high) * scale
    grad_value = jnp.einsum("hrw,rhd->wd", probs_low.astype(jnp.float32), grad_full, precision=high)
    return attended, grad_query, grad_key, grad_value


def reference(queries, keys, values, grad_out, doc_blocks):
    block_ends = (jnp.cumsum(doc_blocks) * 128).astype(jnp.int32)
    reach = SPAN * TOK_DEV
    window = reach + TOK_DEV
    scale = HD ** -0.5

    def one_group(group):
        column = (group * QH_DEV * HD).astype(jnp.int32)
        query_head = lax.dynamic_slice_in_dim(queries, column, QH_DEV * HD, 1).reshape(TOKENS, QH_DEV, HD)
        grad_head = lax.dynamic_slice_in_dim(grad_out, column, QH_DEV * HD, 1).reshape(TOKENS, QH_DEV, HD)
        key_column = (group * HD).astype(jnp.int32)
        key_pad = jnp.pad(lax.dynamic_slice_in_dim(keys, key_column, HD, 1), ((reach, 0), (0, 0)))
        value_pad = jnp.pad(lax.dynamic_slice_in_dim(values, key_column, HD, 1), ((reach, 0), (0, 0)))

        def block_step(carry, block):
            key_sum, value_sum = carry
            start = (block * TOK_DEV).astype(jnp.int32)
            query_rows = lax.dynamic_slice_in_dim(query_head, start, TOK_DEV, 0)
            grad_rows = lax.dynamic_slice_in_dim(grad_head, start, TOK_DEV, 0)
            key_rows = lax.dynamic_slice_in_dim(key_pad, start, window, 0)
            value_rows = lax.dynamic_slice_in_dim(value_pad, start, window, 0)
            query_pos = start + jnp.arange(TOK_DEV, dtype=jnp.int32)
            key_pos = start - reach + jnp.arange(window, dtype=jnp.int32)
            same_doc = segment_of(query_pos, block_ends)[:, None] == segment_of(key_pos, block_ends)[None, :]
            allowed = same_doc & (key_pos[None, :] <= query_pos[:, None])
            attended, grad_query, grad_key, grad_value = attend(query_rows, key_rows, value_rows, grad_rows, allowed, scale)
            key_sum = lax.dynamic_update_slice_in_dim(key_sum, lax.dynamic_slice_in_dim(key_sum, start, window, 0) + grad_key, start, 0)
            value_sum = lax.dynamic_update_slice_in_dim(value_sum, lax.dynamic_slice_in_dim(value_sum, start, window, 0) + grad_value, start, 0)
            return (key_sum, value_sum), (attended.reshape(TOK_DEV, QH_DEV * HD), grad_query.reshape(TOK_DEV, QH_DEV * HD))

        zeros = jnp.zeros((TOKENS + reach, HD), jnp.float32)
        (key_sum, value_sum), (attended, grad_query) = lax.scan(block_step, (zeros, zeros), jnp.arange(N_SEQ, dtype=jnp.int32))
        return (attended.reshape(TOKENS, QH_DEV * HD), grad_query.reshape(TOKENS, QH_DEV * HD),
                key_sum[reach:].astype(jnp.bfloat16), value_sum[reach:].astype(jnp.bfloat16))

    results = lax.map(one_group, jnp.arange(N_HEAD, dtype=jnp.int32))

    def arrange(stacked):
        return jnp.transpose(stacked, (1, 0, 2)).reshape(TOKENS, -1)

    return (arrange(results[0]), arrange(results[1]), arrange(results[2]), arrange(results[3]))
```

```python
import jax
import jax.numpy as jnp
from jax import lax
from jax.experimental import pallas as pl
from jax.experimental.pallas import tpu as pltpu
from jax.sharding import PartitionSpec as P

HD = 128
BLOCK = 128
HEADS = 8
ROWS = 256
SCALE = HD**-0.5
EXP2_SCALE = SCALE * 1.4426950408889634
WINDOW = 9
REACH = 8


def document_start(doc_ref, block):
    end = jnp.int32(0)
    start = jnp.int32(0)
    for doc in range(doc_ref.shape[0]):
        start = jnp.where(end <= block, end, start)
        end = end + doc_ref[doc]
    return start


def attention_kernel(
    doc_ref, qg_ref, mine_ref, theirs_ref,
    att_ref, gq_ref, kept_ref, sent_ref,
    kw, vw, kt, vt, dk, dv,
):
    here = lax.axis_index("seq")
    parity = lax.rem(here, 2)
    far = pl.multiple_of(512 - 256 * parity, 128)
    near = pl.multiple_of(256 - 256 * parity, 128)
    for part, (window, turned) in enumerate(((kw, kt), (vw, vt))):
        at = part * HD
        window[0:128, :] = mine_ref[128:256, 512 + at : 512 + at + HD]
        window[128:384, :] = theirs_ref[:, pl.ds(far + at, HD)]
        window[384:640, :] = mine_ref[:, 256 + at : 256 + at + HD]
        window[640:896, :] = theirs_ref[:, pl.ds(near + at, HD)]
        window[896:1152, :] = mine_ref[:, at : at + HD]
        turned[...] = window[...].T
    dk[...] = jnp.zeros_like(dk)
    dv[...] = jnp.zeros_like(dv)

    starts = [document_start(doc_ref, 2 * here + half) for half in range(2)]
    key_at = lax.broadcasted_iota(jnp.int32, (BLOCK, 2 * BLOCK), 0)
    query_at = lax.rem(lax.broadcasted_iota(jnp.int32, (BLOCK, 2 * BLOCK), 1), BLOCK)
    causal = key_at <= query_at

    def stacked(ref, half, column):
        rows = pl.ds(half * BLOCK, BLOCK)
        return jnp.concatenate(
            [ref[rows, pl.ds(pl.multiple_of(column + i * HD, HD), HD)] for i in range(2)], axis=0
        )

    def pair_of_heads(pair, _):
        column = pair * (2 * HD)
        for half in range(2):
            low, high = half * BLOCK, (half + REACH) * BLOCK
            valid = [
                2 * here - 7 + half + w >= starts[half] for w in range(REACH - 1)
            ]
            q2 = stacked(qg_ref, half, column)
            g2 = stacked(qg_ref, half, HEADS * HD + column)
            qt, gt = q2.T, g2.T
            scores = jnp.dot(kw[low:high, :], qt, preferred_element_type=jnp.float32)
            pieces = [scores[w * BLOCK : (w + 1) * BLOCK, :] for w in range(REACH)]
            pieces[-1] = jnp.where(causal, pieces[-1], -1e30)
            highest = jnp.max(pieces[-1], axis=0, keepdims=True)
            for w in range(REACH - 1):
                top = jnp.max(pieces[w], axis=0, keepdims=True)
                highest = jnp.maximum(highest, jnp.where(valid[w], top, -1e30))
            shift = highest * EXP2_SCALE
            weights = [
                jnp.exp2(
                    piece * EXP2_SCALE
                    - (shift if w == REACH - 1 else jnp.where(valid[w], shift, 1e30))
                )
                for w, piece in enumerate(pieces)
            ]
            weights = jnp.concatenate(weights, axis=0)
            total = jnp.sum(weights, axis=0, keepdims=True)
            probs = weights * (1.0 / total)
            probs_low = probs.astype(jnp.bfloat16)
            att_t = jnp.dot(
                vt[:, low:high], probs_low, preferred_element_type=jnp.float32
            ).astype(jnp.bfloat16)
            delta = jnp.sum(
                gt.astype(jnp.float32) * att_t.astype(jnp.float32), axis=0, keepdims=True
            )
            grad_probs = jnp.dot(vw[low:high, :], gt, preferred_element_type=jnp.float32)
            grad_scores = (probs * (grad_probs - delta)).astype(jnp.bfloat16)
            gq_t = (
                jnp.dot(kt[:, low:high], grad_scores, preferred_element_type=jnp.float32) * SCALE
            ).astype(jnp.bfloat16)
            dv[low:high, :] += jnp.dot(probs_low, g2, preferred_element_type=jnp.float32)
            dk[low:high, :] += jnp.dot(grad_scores, q2, preferred_element_type=jnp.float32)
            rows = pl.ds(half * BLOCK, BLOCK)
            for i in range(2):
                columns = pl.ds(pl.multiple_of(column + i * HD, HD), HD)
                att_ref[rows, columns] = att_t[:, i * BLOCK : (i + 1) * BLOCK].T
                gq_ref[rows, columns] = gq_t[:, i * BLOCK : (i + 1) * BLOCK].T
        return 0

    lax.fori_loop(0, HEADS // 2, pair_of_heads, 0)

    for part, (total, factor) in enumerate(((dk, SCALE), (dv, None))):
        scaled = total[...] if factor is None else total[...] * factor
        at = part * HD
        kept_ref[:, at : at + HD] = scaled[896:1152, :]
        kept_ref[:, 256 + at : 256 + at + HD] = scaled[384:640, :]
        kept_ref[0:128, 512 + at : 512 + at + HD] = jnp.zeros((128, HD), jnp.float32)
        kept_ref[128:256, 512 + at : 512 + at + HD] = scaled[0:128, :]
        sent_ref[:, at : at + HD] = scaled[640:896, :].astype(jnp.bfloat16)
        sent_ref[:, 256 + at : 256 + at + HD] = scaled[128:384, :].astype(jnp.bfloat16)


def attention(doc_blocks, qg, mine, theirs):
    vmem = pl.BlockSpec(memory_space=pltpu.VMEM)
    window = WINDOW * BLOCK
    return pl.pallas_call(
        attention_kernel,
        out_shape=(
            jax.ShapeDtypeStruct((ROWS, HEADS * HD), jnp.bfloat16),
            jax.ShapeDtypeStruct((ROWS, HEADS * HD), jnp.bfloat16),
            jax.ShapeDtypeStruct((ROWS, 6 * HD), jnp.float32),
            jax.ShapeDtypeStruct((ROWS, 4 * HD), jnp.bfloat16),
        ),
        in_specs=[pl.BlockSpec(memory_space=pltpu.SMEM), vmem, vmem, vmem],
        out_specs=(vmem, vmem, vmem, vmem),
        scratch_shapes=[
            pltpu.VMEM((window, HD), jnp.bfloat16),
            pltpu.VMEM((window, HD), jnp.bfloat16),
            pltpu.VMEM((HD, window), jnp.bfloat16),
            pltpu.VMEM((HD, window), jnp.bfloat16),
            pltpu.VMEM((window, HD), jnp.float32),
            pltpu.VMEM((window, HD), jnp.float32),
        ],
        compiler_params=pltpu.CompilerParams(vmem_limit_bytes=40 * 1024 * 1024),
        cost_estimate=pl.CostEstimate(
            flops=3_000_000_000, bytes_accessed=4_000_000, transcendentals=2_100_000
        ),
    )(doc_blocks, qg, mine, theirs)


def shifted(block, distance):
    devices = range(lax.axis_size("seq"))
    route = [(i - distance, i) for i in devices if i - distance in devices]
    return lax.ppermute(block, "seq", route)


def partners(block):
    return lax.ppermute(block, "seq", [(i, i ^ 1) for i in range(lax.axis_size("seq"))])


def by_group(array):
    groups = lax.axis_size("head")
    rows, columns = array.shape
    return jnp.transpose(array.reshape(rows, groups, columns // groups), (1, 0, 2))


def to_groups(chunks):
    received = lax.all_to_all(chunks, "head", split_axis=0, concat_axis=0, tiled=True)
    return received.reshape(-1, chunks.shape[2])


def local(queries, keys, values, grad_out, doc_blocks):
    keys_values = jnp.concatenate([keys, values], axis=1)
    two_back = shifted(keys_values, 2)
    four_back = shifted(keys_values, 4)
    qg = to_groups(jnp.concatenate([by_group(queries), by_group(grad_out)], axis=2))
    width = keys.shape[1]
    mine = to_groups(
        jnp.concatenate(
            [
                by_group(array[:, at : at + width])
                for array in (keys_values, two_back, four_back)
                for at in (0, width)
            ],
            axis=2,
        )
    )
    theirs = partners(mine)
    attended, grad_queries, kept, sent = attention(doc_blocks, qg, mine, theirs)
    odd = lax.rem(lax.axis_index("seq"), 2) == 1
    swapped = partners(sent).astype(jnp.float32)
    one, three = swapped[:, 0:256], swapped[:, 256:512]
    for_here = kept[:, 0:256] + jnp.where(odd, 0.0, one)
    for_two = (kept[:, 256:512] + jnp.where(odd, one, three)).astype(jnp.bfloat16)
    for_four = (kept[:, 512:768] + jnp.where(odd, three, 0.0)).astype(jnp.bfloat16)
    total = (
        for_here
        + shifted(for_two, -2).astype(jnp.float32)
        + shifted(for_four, -4).astype(jnp.float32)
    ).astype(jnp.bfloat16)
    return attended, grad_queries, total[:, 0:128], total[:, 128:256]


def solution(mesh):
    rows = P(("seq", "head"), None)
    return jax.shard_map(
        local,
        mesh=mesh,
        in_specs=(rows, rows, rows, rows, P()),
        out_specs=(P("seq", "head"),) * 4,
        check_vma=False,
    )
```

```python
import jax
import jax.numpy as jnp
from jax import lax
from jax.experimental import pallas as pl
from jax.experimental.pallas import tpu as pltpu
from jax.sharding import PartitionSpec as P

HD = 128
BLOCK = 128
HEADS = 8
ROWS = 256
SCALE = HD**-0.5
EXP2_SCALE = SCALE * 1.4426950408889634
WINDOW = 9
REACH = 8


def document_start(doc_ref, block):
    end = jnp.int32(0)
    start = jnp.int32(0)
    for doc in range(doc_ref.shape[0]):
        start = jnp.where(end <= block, end, start)
        end = end + doc_ref[doc]
    return start


def attention_kernel(
    doc_ref, qg_ref, mine_ref, theirs_ref,
    att_ref, gq_ref, kept_ref, sent_ref,
    kw, vw, kt, vt, dk, dv, scores, weights, grads, qs, gs,
):
    here = lax.axis_index("seq")
    parity = lax.rem(here, 2)
    far = pl.multiple_of(512 - 256 * parity, 128)
    near = pl.multiple_of(256 - 256 * parity, 128)
    for part, (window, turned) in enumerate(((kw, kt), (vw, vt))):
        at = part * HD
        window[0:128, :] = mine_ref[128:256, 512 + at : 512 + at + HD]
        window[128:384, :] = theirs_ref[:, pl.ds(far + at, HD)]
        window[384:640, :] = mine_ref[:, 256 + at : 256 + at + HD]
        window[640:896, :] = theirs_ref[:, pl.ds(near + at, HD)]
        window[896:1152, :] = mine_ref[:, at : at + HD]
        turned[...] = window[...].T
    starts = [document_start(doc_ref, 2 * here + half) for half in range(2)]
    key_at = lax.broadcasted_iota(jnp.int32, (BLOCK, 2 * BLOCK), 0)
    query_at = lax.rem(lax.broadcasted_iota(jnp.int32, (BLOCK, 2 * BLOCK), 1), BLOCK)
    causal = key_at <= query_at

    def stacked(ref, half, column):
        rows = pl.ds(half * BLOCK, BLOCK)
        return jnp.concatenate(
            [ref[rows, pl.ds(column + i * HD, HD)] for i in range(2)], axis=0
        )

    def over_sublanes(op, array):
        return op(array.reshape(BLOCK // 8, 8, 2 * BLOCK), axis=0)

    def pair_of_heads(pair):
        column = pair * (2 * HD)
        for half in range(2):
            low, high = half * BLOCK, (half + REACH) * BLOCK
            valid = [2 * here - 7 + half + w >= starts[half] for w in range(REACH - 1)]
            q2 = stacked(qg_ref, half, column)
            g2 = stacked(qg_ref, half, HEADS * HD + column)
            qt, gt = q2.T, g2.T
            qs[half, pl.ds(column, 2 * BLOCK), :] = q2
            columns = pl.ds(column, 2 * BLOCK)
            highest = None
            for w in range(REACH):
                at = low + w * BLOCK
                score = jnp.dot(kw[at : at + BLOCK, :], qt, preferred_element_type=jnp.float32)
                if w == REACH - 1:
                    score = jnp.where(causal, score, -1e30)
                scores[half, w * BLOCK : (w + 1) * BLOCK, :] = score
                top = over_sublanes(jnp.max, score)
                if w < REACH - 1:
                    top = jnp.where(valid[w], top, -1e30)
                highest = top if highest is None else jnp.maximum(highest, top)
            shift = jnp.max(highest, axis=0, keepdims=True) * EXP2_SCALE
            total = None
            for w in range(REACH):
                rows = pl.ds(w * BLOCK, BLOCK)
                down = shift if w == REACH - 1 else jnp.where(valid[w], shift, 1e30)
                weight = jnp.exp2(scores[half, rows, :] * EXP2_SCALE - down)
                part = over_sublanes(jnp.sum, weight)
                total = part if total is None else total + part
                weights[half, rows, columns] = weight.astype(jnp.bfloat16)
            inverse = 1.0 / jnp.sum(total, axis=0, keepdims=True)
            att_t = (
                jnp.dot(
                    vt[:, low:high], weights[half, :, columns], preferred_element_type=jnp.float32
                )
                * inverse
            ).astype(jnp.bfloat16)
            scaled_t = (gt.astype(jnp.float32) * inverse).astype(jnp.bfloat16)
            gs[half, pl.ds(column, 2 * BLOCK), :] = scaled_t.T
            delta = jnp.sum(
                scaled_t.astype(jnp.float32) * att_t.astype(jnp.float32), axis=0, keepdims=True
            )
            for w in range(REACH):
                at = low + w * BLOCK
                rows = pl.ds(w * BLOCK, BLOCK)
                grad = jnp.dot(
                    vw[at : at + BLOCK, :], scaled_t, preferred_element_type=jnp.float32
                )
                grads[half, rows, columns] = (
                    weights[half, rows, columns].astype(jnp.float32) * (grad - delta)
                ).astype(jnp.bfloat16)
            gq_t = (
                jnp.dot(
                    kt[:, low:high], grads[half, :, columns], preferred_element_type=jnp.float32
                )
                * SCALE
            ).astype(jnp.bfloat16)
            rows = pl.ds(half * BLOCK, BLOCK)
            for i in range(2):
                out = pl.ds(column + i * HD, HD)
                att_ref[rows, out] = att_t[:, i * BLOCK : (i + 1) * BLOCK].T
                gq_ref[rows, out] = gq_t[:, i * BLOCK : (i + 1) * BLOCK].T

    for pair in range(HEADS // 2):
        pair_of_heads(pair)
    for out, left, right in ((dv, weights, gs), (dk, grads, qs)):
        for half in range(2):
            added = jnp.dot(left[half], right[half], preferred_element_type=jnp.float32)
            if half == 0:
                out[0:1024, :] = added
                out[1024:1152, :] = jnp.zeros((BLOCK, HD), jnp.float32)
            else:
                out[128:1152, :] += added

    for part, (total, factor) in enumerate(((dk, SCALE), (dv, None))):
        scaled = total[...] if factor is None else total[...] * factor
        at = part * HD
        kept_ref[:, at : at + HD] = scaled[896:1152, :]
        kept_ref[:, 256 + at : 256 + at + HD] = scaled[384:640, :]
        kept_ref[0:128, 512 + at : 512 + at + HD] = jnp.zeros((128, HD), jnp.float32)
        kept_ref[128:256, 512 + at : 512 + at + HD] = scaled[0:128, :]
        sent_ref[:, at : at + HD] = scaled[640:896, :].astype(jnp.bfloat16)
        sent_ref[:, 256 + at : 256 + at + HD] = scaled[128:384, :].astype(jnp.bfloat16)


def attention(doc_blocks, qg, mine, theirs):
    vmem = pl.BlockSpec(memory_space=pltpu.VMEM)
    window = WINDOW * BLOCK
    return pl.pallas_call(
        attention_kernel,
        out_shape=(
            jax.ShapeDtypeStruct((ROWS, HEADS * HD), jnp.bfloat16),
            jax.ShapeDtypeStruct((ROWS, HEADS * HD), jnp.bfloat16),
            jax.ShapeDtypeStruct((ROWS, 6 * HD), jnp.float32),
            jax.ShapeDtypeStruct((ROWS, 4 * HD), jnp.bfloat16),
        ),
        in_specs=[pl.BlockSpec(memory_space=pltpu.SMEM), vmem, vmem, vmem],
        out_specs=(vmem, vmem, vmem, vmem),
        scratch_shapes=[
            pltpu.VMEM((window, HD), jnp.bfloat16),
            pltpu.VMEM((window, HD), jnp.bfloat16),
            pltpu.VMEM((HD, window), jnp.bfloat16),
            pltpu.VMEM((HD, window), jnp.bfloat16),
            pltpu.VMEM((window, HD), jnp.float32),
            pltpu.VMEM((window, HD), jnp.float32),
            pltpu.VMEM((2, REACH * BLOCK, 2 * BLOCK), jnp.float32),
            pltpu.VMEM((2, REACH * BLOCK, HEADS * BLOCK), jnp.bfloat16),
            pltpu.VMEM((2, REACH * BLOCK, HEADS * BLOCK), jnp.bfloat16),
            pltpu.VMEM((2, HEADS * BLOCK, HD), jnp.bfloat16),
            pltpu.VMEM((2, HEADS * BLOCK, HD), jnp.bfloat16),
        ],
        compiler_params=pltpu.CompilerParams(vmem_limit_bytes=40 * 1024 * 1024),
        cost_estimate=pl.CostEstimate(
            flops=3_000_000_000, bytes_accessed=4_000_000, transcendentals=2_100_000
        ),
    )(doc_blocks, qg, mine, theirs)


def shifted(block, distance):
    devices = range(lax.axis_size("seq"))
    route = [(i - distance, i) for i in devices if i - distance in devices]
    return lax.ppermute(block, "seq", route)


def partners(block):
    return lax.ppermute(block, "seq", [(i, i ^ 1) for i in range(lax.axis_size("seq"))])


def exchanged(chunks):
    received = lax.all_to_all(chunks, "head", split_axis=0, concat_axis=0, tiled=True)
    return received.reshape(-1, chunks.shape[2])


def packing_kernel(queries_ref, grad_out_ref, keys_ref, values_ref, chunks_ref, kv_ref, sems):
    groups, _, width = chunks_ref.shape
    copies = []
    for part, source in enumerate((queries_ref, grad_out_ref)):
        half = width // 2
        for group in range(groups):
            copies.append(
                pltpu.make_async_copy(
                    source.at[:, pl.ds(group * half, half)],
                    chunks_ref.at[group, :, pl.ds(part * half, half)],
                    sems.at[part, group],
                )
            )
    for part, source in enumerate((keys_ref, values_ref)):
        columns = source.shape[1]
        copies.append(
            pltpu.make_async_copy(
                source, kv_ref.at[:, pl.ds(part * columns, columns)], sems.at[2, part]
            )
        )
    for copy in copies:
        copy.start()
    for copy in copies:
        copy.wait()


def packed(queries, keys, values, grad_out):
    groups = lax.axis_size("head")
    rows, columns = queries.shape
    anywhere = pl.BlockSpec(memory_space=pl.ANY)
    return pl.pallas_call(
        packing_kernel,
        out_shape=(
            jax.ShapeDtypeStruct((groups, rows, 2 * columns // groups), queries.dtype),
            jax.ShapeDtypeStruct((rows, 2 * keys.shape[1]), keys.dtype),
        ),
        in_specs=[anywhere] * 4,
        out_specs=(anywhere, anywhere),
        scratch_shapes=[pltpu.SemaphoreType.DMA((3, groups))],
        cost_estimate=pl.CostEstimate(flops=0, bytes_accessed=2_400_000, transcendentals=0),
        compiler_params=pltpu.CompilerParams(vmem_limit_bytes=8 * 1024 * 1024),
    )(queries, grad_out, keys, values)


def piling_kernel(own_ref, two_ref, four_ref, chunks_ref):
    groups, _, width = chunks_ref.shape
    half = own_ref.shape[1] // 2
    for piece, source in enumerate((own_ref, two_ref, four_ref)):
        for part in range(2):
            for group in range(groups):
                at = (2 * piece + part) * HD
                chunks_ref[group, :, at : at + HD] = source[
                    :, part * half + group * HD : part * half + (group + 1) * HD
                ]


def piled(own, two_back, four_back):
    groups = lax.axis_size("head")
    vmem = pl.BlockSpec(memory_space=pltpu.VMEM)
    return pl.pallas_call(
        piling_kernel,
        out_shape=jax.ShapeDtypeStruct((groups, own.shape[0], 6 * HD), own.dtype),
        in_specs=[vmem] * 3,
        out_specs=vmem,
        cost_estimate=pl.CostEstimate(flops=0, bytes_accessed=800_000, transcendentals=0),
        compiler_params=pltpu.CompilerParams(vmem_limit_bytes=8 * 1024 * 1024),
    )(own, two_back, four_back)


def local(queries, keys, values, grad_out, doc_blocks):
    chunks, keys_values = packed(queries, keys, values, grad_out)
    qg = exchanged(chunks)
    two_back = shifted(keys_values, 2)
    four_back = shifted(keys_values, 4)
    pile, qg = lax.optimization_barrier((piled(keys_values, two_back, four_back), qg))
    mine = exchanged(pile)
    theirs = partners(mine)
    attended, grad_queries, kept, sent = attention(doc_blocks, qg, mine, theirs)
    odd = lax.rem(lax.axis_index("seq"), 2) == 1
    swapped = partners(sent).astype(jnp.float32)
    one, three = swapped[:, 0:256], swapped[:, 256:512]
    for_here = kept[:, 0:256] + jnp.where(odd, 0.0, one)
    for_two = (kept[:, 256:512] + jnp.where(odd, one, three)).astype(jnp.bfloat16)
    for_four = (kept[:, 512:768] + jnp.where(odd, three, 0.0)).astype(jnp.bfloat16)
    total = (
        for_here
        + shifted(for_two, -2).astype(jnp.float32)
        + shifted(for_four, -4).astype(jnp.float32)
    ).astype(jnp.bfloat16)
    return attended, grad_queries, total[:, 0:128], total[:, 128:256]


def solution(mesh):
    rows = P(("seq", "head"), None)
    return jax.shard_map(
        local,
        mesh=mesh,
        in_specs=(rows, rows, rows, rows, P()),
        out_specs=(P("seq", "head"),) * 4,
        check_vma=False,
    )
```

```python
import jax
import jax.numpy as jnp
from jax import lax
from jax.experimental import pallas as pl
from jax.experimental.pallas import tpu as pltpu
from jax.sharding import PartitionSpec as P

HD = 128
BLOCK = 128
HEADS = 8
ROWS = 256
SCALE = HD**-0.5
EXP2_SCALE = SCALE * 1.4426950408889634
WINDOW = 9
REACH = 8


def document_start(doc_ref, block):
    end = jnp.int32(0)
    start = jnp.int32(0)
    for doc in range(doc_ref.shape[0]):
        start = jnp.where(end <= block, end, start)
        end = end + doc_ref[doc]
    return start


def attention_kernel(
    doc_ref, qg_ref, own_ref, two_ref, four_ref, their_two_ref, their_other_ref,
    att_ref, gq_ref, kept_ref, sent_ref,
    kw, vw, kt, vt, dk, dv, scores, weights, grads, qs, gs,
):
    here = lax.axis_index("seq")
    parity = lax.rem(here, 2)
    for part, window in enumerate((kw, vw)):
        columns = pl.ds(part * HD, HD)
        window[0:128, :] = four_ref[128:256, columns]
        window[384:640, :] = two_ref[:, columns]
        window[896:1152, :] = own_ref[:, columns]

    @pl.when(parity == 0)
    def _():
        for part, window in enumerate((kw, vw)):
            columns = pl.ds(part * HD, HD)
            window[128:384, :] = their_other_ref[:, columns]
            window[640:896, :] = their_two_ref[:, columns]

    @pl.when(parity == 1)
    def _():
        for part, window in enumerate((kw, vw)):
            columns = pl.ds(part * HD, HD)
            window[128:384, :] = their_two_ref[:, columns]
            window[640:896, :] = their_other_ref[:, columns]

    kt[...] = kw[...].T
    vt[...] = vw[...].T

    starts = [document_start(doc_ref, 2 * here + half) for half in range(2)]
    key_at = lax.broadcasted_iota(jnp.int32, (BLOCK, 2 * BLOCK), 0)
    query_at = lax.rem(lax.broadcasted_iota(jnp.int32, (BLOCK, 2 * BLOCK), 1), BLOCK)
    causal = key_at <= query_at

    def stacked(ref, half, column):
        rows = pl.ds(half * BLOCK, BLOCK)
        return jnp.concatenate(
            [ref[rows, pl.ds(column + i * HD, HD)] for i in range(2)], axis=0
        )

    def over_sublanes(op, array):
        return op(array.reshape(BLOCK // 8, 8, 2 * BLOCK), axis=0)

    def pair_of_heads(pair):
        column = pair * (2 * HD)
        for half in range(2):
            low, high = half * BLOCK, (half + REACH) * BLOCK
            valid = [2 * here - 7 + half + w >= starts[half] for w in range(REACH - 1)]
            q2 = stacked(qg_ref, half, column)
            g2 = stacked(qg_ref, half, HEADS * HD + column)
            qt, gt = q2.T, g2.T
            qs[half, pl.ds(column, 2 * BLOCK), :] = q2
            columns = pl.ds(column, 2 * BLOCK)
            highest = None
            for w in range(REACH):
                at = low + w * BLOCK
                score = jnp.dot(kw[at : at + BLOCK, :], qt, preferred_element_type=jnp.float32)
                if w == REACH - 1:
                    score = jnp.where(causal, score, -1e30)
                scores[half, w * BLOCK : (w + 1) * BLOCK, :] = score
                top = over_sublanes(jnp.max, score)
                if w < REACH - 1:
                    top = jnp.where(valid[w], top, -1e30)
                highest = top if highest is None else jnp.maximum(highest, top)
            shift = jnp.max(highest, axis=0, keepdims=True) * EXP2_SCALE
            total = None
            for w in range(REACH):
                rows = pl.ds(w * BLOCK, BLOCK)
                down = shift if w == REACH - 1 else jnp.where(valid[w], shift, 1e30)
                weight = jnp.exp2(scores[half, rows, :] * EXP2_SCALE - down)
                part = over_sublanes(jnp.sum, weight)
                total = part if total is None else total + part
                weights[half, rows, columns] = weight.astype(jnp.bfloat16)
            inverse = 1.0 / jnp.sum(total, axis=0, keepdims=True)
            att_t = (
                jnp.dot(
                    vt[:, low:high], weights[half, :, columns], preferred_element_type=jnp.float32
                )
                * inverse
            ).astype(jnp.bfloat16)
            scaled_t = (gt.astype(jnp.float32) * inverse).astype(jnp.bfloat16)
            gs[half, pl.ds(column, 2 * BLOCK), :] = scaled_t.T
            delta = jnp.sum(
                scaled_t.astype(jnp.float32) * att_t.astype(jnp.float32), axis=0, keepdims=True
            )
            for w in range(REACH):
                at = low + w * BLOCK
                rows = pl.ds(w * BLOCK, BLOCK)
                grad = jnp.dot(
                    vw[at : at + BLOCK, :], scaled_t, preferred_element_type=jnp.float32
                )
                grads[half, rows, columns] = (
                    weights[half, rows, columns].astype(jnp.float32) * (grad - delta)
                ).astype(jnp.bfloat16)
            gq_t = (
                jnp.dot(
                    kt[:, low:high], grads[half, :, columns], preferred_element_type=jnp.float32
                )
                * SCALE
            ).astype(jnp.bfloat16)
            rows = pl.ds(half * BLOCK, BLOCK)
            for i in range(2):
                out = pl.ds(column + i * HD, HD)
                att_ref[rows, out] = att_t[:, i * BLOCK : (i + 1) * BLOCK].T
                gq_ref[rows, out] = gq_t[:, i * BLOCK : (i + 1) * BLOCK].T

    for pair in range(HEADS // 2):
        pair_of_heads(pair)
    for out, left, right in ((dv, weights, gs), (dk, grads, qs)):
        for half in range(2):
            added = jnp.dot(left[half], right[half], preferred_element_type=jnp.float32)
            if half == 0:
                out[0:1024, :] = added
                out[1024:1152, :] = jnp.zeros((BLOCK, HD), jnp.float32)
            else:
                out[128:1152, :] += added

    for part, (total, factor) in enumerate(((dk, SCALE), (dv, None))):
        scaled = total[...] if factor is None else total[...] * factor
        at = part * HD
        kept_ref[:, at : at + HD] = scaled[896:1152, :]
        kept_ref[:, 256 + at : 256 + at + HD] = scaled[384:640, :]
        kept_ref[0:128, 512 + at : 512 + at + HD] = jnp.zeros((128, HD), jnp.float32)
        kept_ref[128:256, 512 + at : 512 + at + HD] = scaled[0:128, :]
        sent_ref[:, at : at + HD] = scaled[640:896, :].astype(jnp.bfloat16)
        sent_ref[:, 256 + at : 256 + at + HD] = scaled[128:384, :].astype(jnp.bfloat16)


def attention(doc_blocks, qg, *pieces):
    vmem = pl.BlockSpec(memory_space=pltpu.VMEM)
    window = WINDOW * BLOCK
    return pl.pallas_call(
        attention_kernel,
        out_shape=(
            jax.ShapeDtypeStruct((ROWS, HEADS * HD), jnp.bfloat16),
            jax.ShapeDtypeStruct((ROWS, HEADS * HD), jnp.bfloat16),
            jax.ShapeDtypeStruct((ROWS, 6 * HD), jnp.float32),
            jax.ShapeDtypeStruct((ROWS, 4 * HD), jnp.bfloat16),
        ),
        in_specs=[pl.BlockSpec(memory_space=pltpu.SMEM)] + [vmem] * 6,
        out_specs=(vmem, vmem, vmem, vmem),
        scratch_shapes=[
            pltpu.VMEM((window, HD), jnp.bfloat16),
            pltpu.VMEM((window, HD), jnp.bfloat16),
            pltpu.VMEM((HD, window), jnp.bfloat16),
            pltpu.VMEM((HD, window), jnp.bfloat16),
            pltpu.VMEM((window, HD), jnp.float32),
            pltpu.VMEM((window, HD), jnp.float32),
            pltpu.VMEM((2, REACH * BLOCK, 2 * BLOCK), jnp.float32),
            pltpu.VMEM((2, REACH * BLOCK, HEADS * BLOCK), jnp.bfloat16),
            pltpu.VMEM((2, REACH * BLOCK, HEADS * BLOCK), jnp.bfloat16),
            pltpu.VMEM((2, HEADS * BLOCK, HD), jnp.bfloat16),
            pltpu.VMEM((2, HEADS * BLOCK, HD), jnp.bfloat16),
        ],
        compiler_params=pltpu.CompilerParams(vmem_limit_bytes=40 * 1024 * 1024),
        cost_estimate=pl.CostEstimate(
            flops=3_000_000_000, bytes_accessed=4_000_000, transcendentals=2_100_000
        ),
    )(doc_blocks, qg, *pieces)


def shifted(block, distance):
    devices = range(lax.axis_size("seq"))
    route = [(i - distance, i) for i in devices if i - distance in devices]
    return lax.ppermute(block, "seq", route)


def partners(block):
    return lax.ppermute(block, "seq", [(i, i ^ 1) for i in range(lax.axis_size("seq"))])


def exchanged(chunks):
    received = lax.all_to_all(chunks, "head", split_axis=0, concat_axis=0, tiled=True)
    return received.reshape(-1, chunks.shape[2])


def packing_kernel(queries_ref, grad_out_ref, chunks_ref, sems):
    groups, _, width = chunks_ref.shape
    half = width // 2
    copies = [
        pltpu.make_async_copy(
            source.at[:, pl.ds(group * half, half)],
            chunks_ref.at[group, :, pl.ds(part * half, half)],
            sems.at[part, group],
        )
        for part, source in enumerate((queries_ref, grad_out_ref))
        for group in range(groups)
    ]
    for copy in copies:
        copy.start()
    for copy in copies:
        copy.wait()


def packed(queries, grad_out):
    groups = lax.axis_size("head")
    rows, columns = queries.shape
    anywhere = pl.BlockSpec(memory_space=pl.ANY)
    return pl.pallas_call(
        packing_kernel,
        out_shape=jax.ShapeDtypeStruct((groups, rows, 2 * columns // groups), queries.dtype),
        in_specs=[anywhere] * 2,
        out_specs=anywhere,
        scratch_shapes=[pltpu.SemaphoreType.DMA((2, groups))],
        cost_estimate=pl.CostEstimate(flops=0, bytes_accessed=2_100_000, transcendentals=0),
    )(queries, grad_out)


def piling_kernel(keys_ref, values_ref, chunks_ref):
    for group in range(chunks_ref.shape[0]):
        for part, source in enumerate((keys_ref, values_ref)):
            chunks_ref[group, :, part * HD : (part + 1) * HD] = source[
                :, group * HD : (group + 1) * HD
            ]


def piled(keys, values):
    groups = lax.axis_size("head")
    vmem = pl.BlockSpec(memory_space=pltpu.VMEM)
    return pl.pallas_call(
        piling_kernel,
        out_shape=jax.ShapeDtypeStruct((groups, keys.shape[0], 2 * HD), keys.dtype),
        in_specs=[vmem] * 2,
        out_specs=vmem,
        cost_estimate=pl.CostEstimate(flops=0, bytes_accessed=260_000, transcendentals=0),
    )(keys, values)


def local(queries, keys, values, grad_out, doc_blocks):
    odd = lax.rem(lax.axis_index("seq"), 2) == 1
    own = exchanged(piled(keys, values))
    chunks, own = lax.optimization_barrier((packed(queries, grad_out), own))
    qg = exchanged(chunks)
    two = shifted(own, 2)
    four = shifted(own, 4)
    their_two = partners(two)
    their_other = partners(jnp.where(odd, four, own))
    attended, grad_queries, kept, sent = attention(
        doc_blocks, qg, own, two, four, their_two, their_other
    )
    swapped = partners(sent).astype(jnp.float32)
    one, three = swapped[:, 0:256], swapped[:, 256:512]
    for_here = kept[:, 0:256] + jnp.where(odd, 0.0, one)
    for_two = (kept[:, 256:512] + jnp.where(odd, one, three)).astype(jnp.bfloat16)
    for_four = (kept[:, 512:768] + jnp.where(odd, three, 0.0)).astype(jnp.bfloat16)
    total = (
        for_here
        + shifted(for_two, -2).astype(jnp.float32)
        + shifted(for_four, -4).astype(jnp.float32)
    ).astype(jnp.bfloat16)
    return attended, grad_queries, total[:, 0:128], total[:, 128:256]


def solution(mesh):
    rows = P(("seq", "head"), None)
    return jax.shard_map(
        local,
        mesh=mesh,
        in_specs=(rows, rows, rows, rows, P()),
        out_specs=(P("seq", "head"),) * 4,
        check_vma=False,
    )
```

```python
import jax
import jax.numpy as jnp
from jax import lax
from jax.experimental import pallas as pl
from jax.experimental.pallas import tpu as pltpu
from jax.sharding import PartitionSpec as P

HD = 128
BLOCK = 128
HEADS = 8
ROWS = 256
SCALE = HD**-0.5
EXP2_SCALE = SCALE * 1.4426950408889634
WINDOW = 9
REACH = 8


def document_start(doc_ref, block):
    end = jnp.int32(0)
    start = jnp.int32(0)
    for doc in range(doc_ref.shape[0]):
        start = jnp.where(end <= block, end, start)
        end = end + doc_ref[doc]
    return start


def attention_kernel(
    doc_ref, qg_ref, own_ref, two_ref, four_ref, their_two_ref, their_other_ref,
    att_ref, gq_ref, kept_ref, sent_ref,
    kw, vw, kt, vt, dk, dv, scores, weights, grads, qs, gs,
):
    here = lax.axis_index("seq")
    parity = lax.rem(here, 2)
    for part, window in enumerate((kw, vw)):
        columns = pl.ds(part * HD, HD)
        window[0:128, :] = four_ref[128:256, columns]
        window[384:640, :] = two_ref[:, columns]
        window[896:1152, :] = own_ref[:, columns]

    @pl.when(parity == 0)
    def _():
        for part, window in enumerate((kw, vw)):
            columns = pl.ds(part * HD, HD)
            window[128:384, :] = their_other_ref[:, columns]
            window[640:896, :] = their_two_ref[:, columns]

    @pl.when(parity == 1)
    def _():
        for part, window in enumerate((kw, vw)):
            columns = pl.ds(part * HD, HD)
            window[128:384, :] = their_two_ref[:, columns]
            window[640:896, :] = their_other_ref[:, columns]

    kt[...] = kw[...].T
    vt[...] = vw[...].T

    starts = [document_start(doc_ref, 2 * here + half) for half in range(2)]
    key_at = lax.broadcasted_iota(jnp.int32, (BLOCK, 2 * BLOCK), 0)
    query_at = lax.rem(lax.broadcasted_iota(jnp.int32, (BLOCK, 2 * BLOCK), 1), BLOCK)
    causal = key_at <= query_at

    def stacked(ref, half, column):
        rows = pl.ds(half * BLOCK, BLOCK)
        return jnp.concatenate(
            [ref[rows, pl.ds(column + i * HD, HD)] for i in range(2)], axis=0
        )

    def over_sublanes(op, array):
        return op(array.reshape(BLOCK // 8, 8, 2 * BLOCK), axis=0)

    def pair_of_heads(pair):
        column = pair * (2 * HD)
        for half in range(2):
            low, high = half * BLOCK, (half + REACH) * BLOCK
            valid = [2 * here - 7 + half + w >= starts[half] for w in range(REACH - 1)]
            q2 = stacked(qg_ref, half, column)
            g2 = stacked(qg_ref, half, HEADS * HD + column)
            qt, gt = q2.T, g2.T
            qs[half, pl.ds(column, 2 * BLOCK), :] = q2
            columns = pl.ds(column, 2 * BLOCK)
            highest = None
            for w in range(REACH):
                at = low + w * BLOCK
                score = jnp.dot(kw[at : at + BLOCK, :], qt, preferred_element_type=jnp.float32)
                if w == REACH - 1:
                    score = jnp.where(causal, score, -1e30)
                scores[half, w * BLOCK : (w + 1) * BLOCK, :] = score
                top = over_sublanes(jnp.max, score)
                if w < REACH - 1:
                    top = jnp.where(valid[w], top, -1e30)
                highest = top if highest is None else jnp.maximum(highest, top)
            shift = jnp.max(highest, axis=0, keepdims=True) * EXP2_SCALE
            total = None
            for w in range(REACH):
                rows = pl.ds(w * BLOCK, BLOCK)
                down = shift if w == REACH - 1 else jnp.where(valid[w], shift, 1e30)
                weight = jnp.exp2(scores[half, rows, :] * EXP2_SCALE - down)
                part = over_sublanes(jnp.sum, weight)
                total = part if total is None else total + part
                weights[half, rows, columns] = weight.astype(jnp.bfloat16)
            inverse = 1.0 / jnp.sum(total, axis=0, keepdims=True)
            att_t = (
                jnp.dot(
                    vt[:, low:high], weights[half, :, columns], preferred_element_type=jnp.float32
                )
                * inverse
            ).astype(jnp.bfloat16)
            scaled_t = (gt.astype(jnp.float32) * inverse).astype(jnp.bfloat16)
            gs[half, pl.ds(column, 2 * BLOCK), :] = scaled_t.T
            delta = jnp.sum(
                scaled_t.astype(jnp.float32) * att_t.astype(jnp.float32), axis=0, keepdims=True
            )
            for w in range(REACH):
                at = low + w * BLOCK
                rows = pl.ds(w * BLOCK, BLOCK)
                grad = jnp.dot(
                    vw[at : at + BLOCK, :], scaled_t, preferred_element_type=jnp.float32
                )
                grads[half, rows, columns] = (
                    weights[half, rows, columns].astype(jnp.float32) * (grad - delta)
                ).astype(jnp.bfloat16)
            gq_t = (
                jnp.dot(
                    kt[:, low:high], grads[half, :, columns], preferred_element_type=jnp.float32
                )
                * SCALE
            ).astype(jnp.bfloat16)
            rows = pl.ds(half * BLOCK, BLOCK)
            for i in range(2):
                out = pl.ds(column + i * HD, HD)
                att_ref[rows, out] = att_t[:, i * BLOCK : (i + 1) * BLOCK].T
                gq_ref[rows, out] = gq_t[:, i * BLOCK : (i + 1) * BLOCK].T

    for pair in range(HEADS // 2):
        pair_of_heads(pair)
    for out, left, right in ((dv, weights, gs), (dk, grads, qs)):
        for half in range(2):
            added = jnp.dot(left[half], right[half], preferred_element_type=jnp.float32)
            if half == 0:
                out[0:1024, :] = added
                out[1024:1152, :] = jnp.zeros((BLOCK, HD), jnp.float32)
            else:
                out[128:1152, :] += added

    for part, (total, factor) in enumerate(((dk, SCALE), (dv, None))):
        scaled = total[...] if factor is None else total[...] * factor
        at = part * HD
        kept_ref[:, at : at + HD] = scaled[896:1152, :]
        kept_ref[:, 256 + at : 256 + at + HD] = scaled[384:640, :]
        kept_ref[0:128, 512 + at : 512 + at + HD] = jnp.zeros((128, HD), jnp.float32)
        kept_ref[128:256, 512 + at : 512 + at + HD] = scaled[0:128, :]
        sent_ref[:, at : at + HD] = scaled[640:896, :].astype(jnp.bfloat16)
        sent_ref[:, 256 + at : 256 + at + HD] = scaled[128:384, :].astype(jnp.bfloat16)


def attention(doc_blocks, qg, *pieces):
    vmem = pl.BlockSpec(memory_space=pltpu.VMEM)
    window = WINDOW * BLOCK
    return pl.pallas_call(
        attention_kernel,
        out_shape=(
            jax.ShapeDtypeStruct((ROWS, HEADS * HD), jnp.bfloat16),
            jax.ShapeDtypeStruct((ROWS, HEADS * HD), jnp.bfloat16),
            jax.ShapeDtypeStruct((ROWS, 6 * HD), jnp.float32),
            jax.ShapeDtypeStruct((ROWS, 4 * HD), jnp.bfloat16),
        ),
        in_specs=[pl.BlockSpec(memory_space=pltpu.SMEM)] + [vmem] * 6,
        out_specs=(vmem, vmem, vmem, vmem),
        scratch_shapes=[
            pltpu.VMEM((window, HD), jnp.bfloat16),
            pltpu.VMEM((window, HD), jnp.bfloat16),
            pltpu.VMEM((HD, window), jnp.bfloat16),
            pltpu.VMEM((HD, window), jnp.bfloat16),
            pltpu.VMEM((window, HD), jnp.float32),
            pltpu.VMEM((window, HD), jnp.float32),
            pltpu.VMEM((2, REACH * BLOCK, 2 * BLOCK), jnp.float32),
            pltpu.VMEM((2, REACH * BLOCK, HEADS * BLOCK), jnp.bfloat16),
            pltpu.VMEM((2, REACH * BLOCK, HEADS * BLOCK), jnp.bfloat16),
            pltpu.VMEM((2, HEADS * BLOCK, HD), jnp.bfloat16),
            pltpu.VMEM((2, HEADS * BLOCK, HD), jnp.bfloat16),
        ],
        compiler_params=pltpu.CompilerParams(vmem_limit_bytes=40 * 1024 * 1024),
        cost_estimate=pl.CostEstimate(
            flops=3_000_000_000, bytes_accessed=4_000_000, transcendentals=2_100_000
        ),
    )(doc_blocks, qg, *pieces)


def shifted(block, distance):
    devices = range(lax.axis_size("seq"))
    route = [(i - distance, i) for i in devices if i - distance in devices]
    return lax.ppermute(block, "seq", route)


def partners(block):
    return lax.ppermute(block, "seq", [(i, i ^ 1) for i in range(lax.axis_size("seq"))])


def exchanged(chunks):
    received = lax.all_to_all(chunks, "head", split_axis=0, concat_axis=0, tiled=True)
    return received.reshape(-1, chunks.shape[2])


def packing_kernel(queries_ref, grad_out_ref, chunks_ref, held, in_sems, out_sems):
    groups, _, width = chunks_ref.shape
    half = width // 2

    def arriving(part, group):
        source = (queries_ref, grad_out_ref)[part]
        return pltpu.make_async_copy(
            source.at[:, pl.ds(group * half, half)],
            held.at[group, :, pl.ds(part * half, half)],
            in_sems.at[part, group],
        )

    def leaving(group):
        return pltpu.make_async_copy(held.at[group], chunks_ref.at[group], out_sems.at[group])

    for group in range(groups):
        for part in range(2):
            arriving(part, group).start()
    for group in range(groups):
        for part in range(2):
            arriving(part, group).wait()
        leaving(group).start()
    for group in range(groups):
        leaving(group).wait()


def packed(queries, grad_out):
    groups = lax.axis_size("head")
    rows, columns = queries.shape
    chunks = (groups, rows, 2 * columns // groups)
    anywhere = pl.BlockSpec(memory_space=pl.ANY)
    return pl.pallas_call(
        packing_kernel,
        out_shape=jax.ShapeDtypeStruct(chunks, queries.dtype),
        in_specs=[anywhere] * 2,
        out_specs=anywhere,
        scratch_shapes=[
            pltpu.VMEM(chunks, queries.dtype),
            pltpu.SemaphoreType.DMA((2, groups)),
            pltpu.SemaphoreType.DMA((groups,)),
        ],
        cost_estimate=pl.CostEstimate(flops=0, bytes_accessed=2_100_000, transcendentals=0),
    )(queries, grad_out)


def piling_kernel(keys_ref, values_ref, chunks_ref):
    for group in range(chunks_ref.shape[0]):
        for part, source in enumerate((keys_ref, values_ref)):
            chunks_ref[group, :, part * HD : (part + 1) * HD] = source[
                :, group * HD : (group + 1) * HD
            ]


def piled(keys, values):
    groups = lax.axis_size("head")
    vmem = pl.BlockSpec(memory_space=pltpu.VMEM)
    return pl.pallas_call(
        piling_kernel,
        out_shape=jax.ShapeDtypeStruct((groups, keys.shape[0], 2 * HD), keys.dtype),
        in_specs=[vmem] * 2,
        out_specs=vmem,
        cost_estimate=pl.CostEstimate(flops=0, bytes_accessed=260_000, transcendentals=0),
    )(keys, values)


def local(queries, keys, values, grad_out, doc_blocks):
    odd = lax.rem(lax.axis_index("seq"), 2) == 1
    own = exchanged(piled(keys, values))
    chunks, own = lax.optimization_barrier((packed(queries, grad_out), own))
    qg = exchanged(chunks)
    two = shifted(own, 2)
    four = shifted(own, 4)
    their_two = partners(two)
    their_other = partners(jnp.where(odd, four, own))
    attended, grad_queries, kept, sent = attention(
        doc_blocks, qg, own, two, four, their_two, their_other
    )
    swapped = partners(sent).astype(jnp.float32)
    one, three = swapped[:, 0:256], swapped[:, 256:512]
    for_here = kept[:, 0:256] + jnp.where(odd, 0.0, one)
    for_two = (kept[:, 256:512] + jnp.where(odd, one, three)).astype(jnp.bfloat16)
    for_four = (kept[:, 512:768] + jnp.where(odd, three, 0.0)).astype(jnp.bfloat16)
    total = (
        for_here
        + shifted(for_two, -2).astype(jnp.float32)
        + shifted(for_four, -4).astype(jnp.float32)
    ).astype(jnp.bfloat16)
    return attended, grad_queries, total[:, 0:128], total[:, 128:256]


def solution(mesh):
    rows = P(("seq", "head"), None)
    return jax.shard_map(
        local,
        mesh=mesh,
        in_specs=(rows, rows, rows, rows, P()),
        out_specs=(P("seq", "head"),) * 4,
        check_vma=False,
    )
```

```python
import functools

import jax
import jax.numpy as jnp
from jax import lax
from jax.experimental import pallas as pl
from jax.experimental.pallas import tpu as pltpu
from jax.sharding import PartitionSpec as P

HD = 128
BLOCK = 128
HEADS = 8
ROWS = 256
SCALE = HD**-0.5
EXP2_SCALE = SCALE * 1.4426950408889634
WINDOW = 9
REACH = 8
REACHES = (2, 4, 6, 8)


def document_start(doc_ref, block):
    end = jnp.int32(0)
    start = jnp.int32(0)
    for doc in range(doc_ref.shape[0]):
        start = jnp.where(end <= block, end, start)
        end = end + doc_ref[doc]
    return start


def attention_kernel(
    doc_ref, qg_ref, own_ref, two_ref, four_ref, their_two_ref, their_other_ref,
    att_ref, gq_ref, kept_ref, sent_ref,
    kw, vw, kt, vt, dk, dv, scores, weights, grads, qs, gs,
):
    here = lax.axis_index("seq")
    parity = lax.rem(here, 2)
    for part, window in enumerate((kw, vw)):
        columns = pl.ds(part * HD, HD)
        window[0:128, :] = four_ref[128:256, columns]
        window[384:640, :] = two_ref[:, columns]
        window[896:1152, :] = own_ref[:, columns]

    @pl.when(parity == 0)
    def _():
        for part, window in enumerate((kw, vw)):
            columns = pl.ds(part * HD, HD)
            window[128:384, :] = their_other_ref[:, columns]
            window[640:896, :] = their_two_ref[:, columns]

    @pl.when(parity == 1)
    def _():
        for part, window in enumerate((kw, vw)):
            columns = pl.ds(part * HD, HD)
            window[128:384, :] = their_two_ref[:, columns]
            window[640:896, :] = their_other_ref[:, columns]

    kt[...] = kw[...].T
    vt[...] = vw[...].T

    starts = [document_start(doc_ref, 2 * here + half) for half in range(2)]
    key_at = lax.broadcasted_iota(jnp.int32, (BLOCK, 2 * BLOCK), 0)
    query_at = lax.rem(lax.broadcasted_iota(jnp.int32, (BLOCK, 2 * BLOCK), 1), BLOCK)
    causal = key_at <= query_at

    def stacked(ref, half, column):
        rows = pl.ds(half * BLOCK, BLOCK)
        return jnp.concatenate(
            [ref[rows, pl.ds(column + i * HD, HD)] for i in range(2)], axis=0
        )

    def over_sublanes(op, array):
        return op(array.reshape(-1, 8, 2 * BLOCK), axis=0)

    class Unit:
        def __init__(self, number, reach):
            self.pair, self.half = divmod(number, 2)
            self.slot = number % 2
            self.column = self.pair * 2 * HD
            self.columns = pl.ds(self.column, 2 * BLOCK)
            self.low = (self.half + REACH - reach) * BLOCK
            self.high = (self.half + REACH) * BLOCK
            self.rows = pl.ds((REACH - reach) * BLOCK, reach * BLOCK)

        def valid(self, w):
            return 2 * here - 7 + self.half + w >= starts[self.half]

        def load(self):
            q2 = stacked(qg_ref, self.half, self.column)
            self.qt = q2.T
            self.gt = stacked(qg_ref, self.half, HEADS * HD + self.column).T
            qs[self.half, self.columns, :] = q2
            self.highest = None

        def score(self, w):
            at = (self.half + w) * BLOCK
            score = jnp.dot(kw[at : at + BLOCK, :], self.qt, preferred_element_type=jnp.float32)
            if w == REACH - 1:
                score = jnp.where(causal, score, -1e30)
            scores[self.slot, w * BLOCK : (w + 1) * BLOCK, :] = score
            top = over_sublanes(jnp.max, score)
            if w < REACH - 1:
                top = jnp.where(self.valid(w), top, -1e30)
            self.highest = top if self.highest is None else jnp.maximum(self.highest, top)

        def level(self):
            self.shift = jnp.max(self.highest, axis=0, keepdims=True) * EXP2_SCALE
            self.total = None

        def weigh(self, w):
            rows = pl.ds(w * BLOCK, BLOCK)
            down = self.shift if w == REACH - 1 else jnp.where(self.valid(w), self.shift, 1e30)
            weight = jnp.exp2(scores[self.slot, rows, :] * EXP2_SCALE - down)
            part = over_sublanes(jnp.sum, weight)
            self.total = part if self.total is None else self.total + part
            weights[self.half, rows, self.columns] = weight.astype(jnp.bfloat16)

        def attend(self):
            inverse = 1.0 / jnp.sum(self.total, axis=0, keepdims=True)
            att_t = (
                jnp.dot(
                    vt[:, self.low : self.high],
                    weights[self.half, self.rows, self.columns],
                    preferred_element_type=jnp.float32,
                )
                * inverse
            ).astype(jnp.bfloat16)
            self.scaled_t = (self.gt.astype(jnp.float32) * inverse).astype(jnp.bfloat16)
            gs[self.half, self.columns, :] = self.scaled_t.T
            self.delta = jnp.sum(
                self.scaled_t.astype(jnp.float32) * att_t.astype(jnp.float32),
                axis=0,
                keepdims=True,
            )
            self.store(att_ref, att_t)

        def grade(self, w):
            at = (self.half + w) * BLOCK
            rows = pl.ds(w * BLOCK, BLOCK)
            grad = jnp.dot(
                vw[at : at + BLOCK, :], self.scaled_t, preferred_element_type=jnp.float32
            )
            grads[self.half, rows, self.columns] = (
                weights[self.half, rows, self.columns].astype(jnp.float32) * (grad - self.delta)
            ).astype(jnp.bfloat16)

        def finish(self):
            gq_t = (
                jnp.dot(
                    kt[:, self.low : self.high],
                    grads[self.half, self.rows, self.columns],
                    preferred_element_type=jnp.float32,
                )
                * SCALE
            ).astype(jnp.bfloat16)
            self.store(gq_ref, gq_t)

        def store(self, ref, turned):
            for i in range(2):
                ref[
                    pl.ds(self.half * BLOCK, BLOCK), pl.ds(self.column + i * HD, HD)
                ] = turned[:, i * BLOCK : (i + 1) * BLOCK].T

    def work(reach):
        units = [Unit(number, reach) for number in range(HEADS)]
        for step in range(len(units) + 2):
            first, second, third = (
                units[step - lag] if 0 <= step - lag < len(units) else None for lag in range(3)
            )
            if first:
                first.load()
            if second:
                second.level()
            for w in range(REACH - reach, REACH):
                if first:
                    first.score(w)
                if second:
                    second.weigh(w)
                if third:
                    third.grade(w)
            if second:
                second.attend()
            if third:
                third.finish()
        begin = (REACH - reach) * BLOCK
        for out, left, right in ((dv, weights, gs), (dk, grads, qs)):
            for half in range(2):
                added = jnp.dot(
                    left[half, begin : REACH * BLOCK, :],
                    right[half],
                    preferred_element_type=jnp.float32,
                )
                if half == 0:
                    if begin:
                        out[0:begin, :] = jnp.zeros((begin, HD), jnp.float32)
                    out[begin : REACH * BLOCK, :] = added
                    out[REACH * BLOCK :, :] = jnp.zeros((BLOCK, HD), jnp.float32)
                else:
                    out[begin + BLOCK :, :] += added

    needed = jnp.maximum(2 * here - starts[0], 2 * here + 1 - starts[1]) + 1
    for number, reach in enumerate(REACHES):
        below = REACHES[number - 1] if number else 0
        pl.when((needed > below) & (needed <= reach))(functools.partial(work, reach))

    for part, (total, factor) in enumerate(((dk, SCALE), (dv, None))):
        scaled = total[...] if factor is None else total[...] * factor
        at = part * HD
        kept_ref[:, at : at + HD] = scaled[896:1152, :]
        kept_ref[:, 256 + at : 256 + at + HD] = scaled[384:640, :]
        kept_ref[0:128, 512 + at : 512 + at + HD] = jnp.zeros((128, HD), jnp.float32)
        kept_ref[128:256, 512 + at : 512 + at + HD] = scaled[0:128, :]
        sent_ref[:, at : at + HD] = scaled[640:896, :].astype(jnp.bfloat16)
        sent_ref[:, 256 + at : 256 + at + HD] = scaled[128:384, :].astype(jnp.bfloat16)


def attention(doc_blocks, qg, *pieces):
    vmem = pl.BlockSpec(memory_space=pltpu.VMEM)
    window = WINDOW * BLOCK
    return pl.pallas_call(
        attention_kernel,
        out_shape=(
            jax.ShapeDtypeStruct((ROWS, HEADS * HD), jnp.bfloat16),
            jax.ShapeDtypeStruct((ROWS, HEADS * HD), jnp.bfloat16),
            jax.ShapeDtypeStruct((ROWS, 6 * HD), jnp.float32),
            jax.ShapeDtypeStruct((ROWS, 4 * HD), jnp.bfloat16),
        ),
        in_specs=[pl.BlockSpec(memory_space=pltpu.SMEM)] + [vmem] * 6,
        out_specs=(vmem, vmem, vmem, vmem),
        scratch_shapes=[
            pltpu.VMEM((window, HD), jnp.bfloat16),
            pltpu.VMEM((window, HD), jnp.bfloat16),
            pltpu.VMEM((HD, window), jnp.bfloat16),
            pltpu.VMEM((HD, window), jnp.bfloat16),
            pltpu.VMEM((window, HD), jnp.float32),
            pltpu.VMEM((window, HD), jnp.float32),
            pltpu.VMEM((2, REACH * BLOCK, 2 * BLOCK), jnp.float32),
            pltpu.VMEM((2, REACH * BLOCK, HEADS * BLOCK), jnp.bfloat16),
            pltpu.VMEM((2, REACH * BLOCK, HEADS * BLOCK), jnp.bfloat16),
            pltpu.VMEM((2, HEADS * BLOCK, HD), jnp.bfloat16),
            pltpu.VMEM((2, HEADS * BLOCK, HD), jnp.bfloat16),
        ],
        compiler_params=pltpu.CompilerParams(vmem_limit_bytes=40 * 1024 * 1024),
        cost_estimate=pl.CostEstimate(
            flops=3_000_000_000, bytes_accessed=4_000_000, transcendentals=2_100_000
        ),
    )(doc_blocks, qg, *pieces)


def shifted(block, distance):
    devices = range(lax.axis_size("seq"))
    route = [(i - distance, i) for i in devices if i - distance in devices]
    return lax.ppermute(block, "seq", route)


def partners(block):
    return lax.ppermute(block, "seq", [(i, i ^ 1) for i in range(lax.axis_size("seq"))])


def exchanged(chunks):
    received = lax.all_to_all(chunks, "head", split_axis=0, concat_axis=0, tiled=True)
    return received.reshape(-1, chunks.shape[2])


def packing_kernel(queries_ref, grad_out_ref, chunks_ref, held, in_sems, out_sems):
    groups, _, width = chunks_ref.shape
    half = width // 2

    def arriving(part, group):
        source = (queries_ref, grad_out_ref)[part]
        return pltpu.make_async_copy(
            source.at[:, pl.ds(group * half, half)],
            held.at[group, :, pl.ds(part * half, half)],
            in_sems.at[part, group],
        )

    def leaving(group):
        return pltpu.make_async_copy(held.at[group], chunks_ref.at[group], out_sems.at[group])

    for group in range(groups):
        for part in range(2):
            arriving(part, group).start()
    for group in range(groups):
        for part in range(2):
            arriving(part, group).wait()
        leaving(group).start()
    for group in range(groups):
        leaving(group).wait()


def packed(queries, grad_out):
    groups = lax.axis_size("head")
    rows, columns = queries.shape
    chunks = (groups, rows, 2 * columns // groups)
    anywhere = pl.BlockSpec(memory_space=pl.ANY)
    return pl.pallas_call(
        packing_kernel,
        out_shape=jax.ShapeDtypeStruct(chunks, queries.dtype),
        in_specs=[anywhere] * 2,
        out_specs=anywhere,
        scratch_shapes=[
            pltpu.VMEM(chunks, queries.dtype),
            pltpu.SemaphoreType.DMA((2, groups)),
            pltpu.SemaphoreType.DMA((groups,)),
        ],
        cost_estimate=pl.CostEstimate(flops=0, bytes_accessed=2_100_000, transcendentals=0),
    )(queries, grad_out)


def piling_kernel(keys_ref, values_ref, chunks_ref):
    for group in range(chunks_ref.shape[0]):
        for part, source in enumerate((keys_ref, values_ref)):
            chunks_ref[group, :, part * HD : (part + 1) * HD] = source[
                :, group * HD : (group + 1) * HD
            ]


def piled(keys, values):
    groups = lax.axis_size("head")
    vmem = pl.BlockSpec(memory_space=pltpu.VMEM)
    return pl.pallas_call(
        piling_kernel,
        out_shape=jax.ShapeDtypeStruct((groups, keys.shape[0], 2 * HD), keys.dtype),
        in_specs=[vmem] * 2,
        out_specs=vmem,
        cost_estimate=pl.CostEstimate(flops=0, bytes_accessed=260_000, transcendentals=0),
    )(keys, values)


def local(queries, keys, values, grad_out, doc_blocks):
    odd = lax.rem(lax.axis_index("seq"), 2) == 1
    own = exchanged(piled(keys, values))
    chunks, own = lax.optimization_barrier((packed(queries, grad_out), own))
    qg = exchanged(chunks)
    two = shifted(own, 2)
    four = shifted(own, 4)
    their_two = partners(two)
    their_other = partners(jnp.where(odd, four, own))
    attended, grad_queries, kept, sent = attention(
        doc_blocks, qg, own, two, four, their_two, their_other
    )
    swapped = partners(sent).astype(jnp.float32)
    one, three = swapped[:, 0:256], swapped[:, 256:512]
    for_here = kept[:, 0:256] + jnp.where(odd, 0.0, one)
    for_two = (kept[:, 256:512] + jnp.where(odd, one, three)).astype(jnp.bfloat16)
    for_four = (kept[:, 512:768] + jnp.where(odd, three, 0.0)).astype(jnp.bfloat16)
    total = (
        for_here
        + shifted(for_two, -2).astype(jnp.float32)
        + shifted(for_four, -4).astype(jnp.float32)
    ).astype(jnp.bfloat16)
    return attended, grad_queries, total[:, 0:128], total[:, 128:256]


def solution(mesh):
    rows = P(("seq", "head"), None)
    return jax.shard_map(
        local,
        mesh=mesh,
        in_specs=(rows, rows, rows, rows, P()),
        out_specs=(P("seq", "head"),) * 4,
        check_vma=False,
    )
```

```python
import functools

import jax
import jax.numpy as jnp
from jax import lax
from jax.experimental import pallas as pl
from jax.experimental.pallas import tpu as pltpu
from jax.sharding import PartitionSpec as P

HD = 128
BLOCK = 128
HEADS = 8
ROWS = 256
SCALE = HD**-0.5
EXP2_SCALE = SCALE * 1.4426950408889634
WINDOW = 9
REACH = 8
REACHES = (2, 4, 6, 8)


def document_start(doc_ref, block):
    end = jnp.int32(0)
    start = jnp.int32(0)
    for doc in range(doc_ref.shape[0]):
        start = jnp.where(end <= block, end, start)
        end = end + doc_ref[doc]
    return start


def attention_kernel(
    doc_ref, qg_ref, own_ref, two_ref, four_ref, their_two_ref, their_other_ref,
    att_ref, gq_ref, kept_ref, sent_ref,
    kw, vw, kt, vt, dk, dv, scores, weights, grads, qs, gs,
):
    here = lax.axis_index("seq")
    parity = lax.rem(here, 2)
    for part, window in enumerate((kw, vw)):
        columns = pl.ds(part * HD, HD)
        window[0:128, :] = four_ref[128:256, columns]
        window[384:640, :] = two_ref[:, columns]
        window[896:1152, :] = own_ref[:, columns]

    @pl.when(parity == 0)
    def _():
        for part, window in enumerate((kw, vw)):
            columns = pl.ds(part * HD, HD)
            window[128:384, :] = their_other_ref[:, columns]
            window[640:896, :] = their_two_ref[:, columns]

    @pl.when(parity == 1)
    def _():
        for part, window in enumerate((kw, vw)):
            columns = pl.ds(part * HD, HD)
            window[128:384, :] = their_two_ref[:, columns]
            window[640:896, :] = their_other_ref[:, columns]

    kt[...] = kw[...].T
    vt[...] = vw[...].T

    starts = [document_start(doc_ref, 2 * here + half) for half in range(2)]
    key_at = lax.broadcasted_iota(jnp.int32, (BLOCK, 2 * BLOCK), 0)
    query_at = lax.rem(lax.broadcasted_iota(jnp.int32, (BLOCK, 2 * BLOCK), 1), BLOCK)
    causal = key_at <= query_at

    def stacked(ref, half, column):
        rows = pl.ds(half * BLOCK, BLOCK)
        return jnp.concatenate(
            [ref[rows, pl.ds(column + i * HD, HD)] for i in range(2)], axis=0
        )

    def over_sublanes(op, array):
        return op(array.reshape(-1, 8, 2 * BLOCK), axis=0)

    class Unit:
        def __init__(self, number, reach):
            self.pair, self.half = divmod(number, 2)
            self.slot = number % 2
            self.column = self.pair * 2 * HD
            self.columns = pl.ds(self.column, 2 * BLOCK)
            self.low = (self.half + REACH - reach) * BLOCK
            self.high = (self.half + REACH) * BLOCK
            self.rows = pl.ds((REACH - reach) * BLOCK, reach * BLOCK)

        def valid(self, w):
            return 2 * here - 7 + self.half + w >= starts[self.half]

        def load(self):
            q2 = stacked(qg_ref, self.half, self.column)
            self.qt = q2.T
            self.gt = stacked(qg_ref, self.half, HEADS * HD + self.column).T
            qs[self.half, self.columns, :] = q2
            self.highest = None

        def score(self, w):
            at = (self.half + w) * BLOCK
            score = jnp.dot(kw[at : at + BLOCK, :], self.qt, preferred_element_type=jnp.float32)
            if w == REACH - 1:
                score = jnp.where(causal, score, -1e30)
            scores[self.slot, w * BLOCK : (w + 1) * BLOCK, :] = score
            top = over_sublanes(jnp.max, score)
            if w < REACH - 1:
                top = jnp.where(self.valid(w), top, -1e30)
            self.highest = top if self.highest is None else jnp.maximum(self.highest, top)

        def level(self):
            self.shift = jnp.max(self.highest, axis=0, keepdims=True) * EXP2_SCALE
            self.total = None

        def weigh(self, w):
            rows = pl.ds(w * BLOCK, BLOCK)
            down = self.shift if w == REACH - 1 else jnp.where(self.valid(w), self.shift, 1e30)
            weight = jnp.exp2(scores[self.slot, rows, :] * EXP2_SCALE - down)
            part = over_sublanes(jnp.sum, weight)
            self.total = part if self.total is None else self.total + part
            weights[self.half, rows, self.columns] = weight.astype(jnp.bfloat16)

        def attend(self):
            inverse = 1.0 / jnp.sum(self.total, axis=0, keepdims=True)
            att_t = (
                jnp.dot(
                    vt[:, self.low : self.high],
                    weights[self.half, self.rows, self.columns],
                    preferred_element_type=jnp.float32,
                )
                * inverse
            ).astype(jnp.bfloat16)
            self.scaled_t = (self.gt.astype(jnp.float32) * inverse).astype(jnp.bfloat16)
            gs[self.half, self.columns, :] = self.scaled_t.T
            self.delta = jnp.sum(
                self.scaled_t.astype(jnp.float32) * att_t.astype(jnp.float32),
                axis=0,
                keepdims=True,
            )
            self.store(att_ref, att_t)

        def grade(self, w):
            at = (self.half + w) * BLOCK
            rows = pl.ds(w * BLOCK, BLOCK)
            grad = jnp.dot(
                vw[at : at + BLOCK, :], self.scaled_t, preferred_element_type=jnp.float32
            )
            grads[self.half, rows, self.columns] = (
                weights[self.half, rows, self.columns].astype(jnp.float32) * (grad - self.delta)
            ).astype(jnp.bfloat16)

        def finish(self):
            gq_t = (
                jnp.dot(
                    kt[:, self.low : self.high],
                    grads[self.half, self.rows, self.columns],
                    preferred_element_type=jnp.float32,
                )
                * SCALE
            ).astype(jnp.bfloat16)
            self.store(gq_ref, gq_t)

        def store(self, ref, turned):
            for i in range(2):
                ref[
                    pl.ds(self.half * BLOCK, BLOCK), pl.ds(self.column + i * HD, HD)
                ] = turned[:, i * BLOCK : (i + 1) * BLOCK].T

    def work(reach):
        units = [Unit(number, reach) for number in range(HEADS)]
        for step in range(len(units) + 2):
            first, second, third = (
                units[step - lag] if 0 <= step - lag < len(units) else None for lag in range(3)
            )
            if first:
                first.load()
            if second:
                second.level()
            for w in range(REACH - reach, REACH):
                if first:
                    first.score(w)
                if second:
                    second.weigh(w)
                if third:
                    third.grade(w)
            if second:
                second.attend()
            if third:
                third.finish()
        begin = (REACH - reach) * BLOCK
        for out, left, right in ((dv, weights, gs), (dk, grads, qs)):
            for half in range(2):
                added = jnp.dot(
                    left[half, begin : REACH * BLOCK, :],
                    right[half],
                    preferred_element_type=jnp.float32,
                )
                if half == 0:
                    if begin:
                        out[0:begin, :] = jnp.zeros((begin, HD), jnp.float32)
                    out[begin : REACH * BLOCK, :] = added
                    out[REACH * BLOCK :, :] = jnp.zeros((BLOCK, HD), jnp.float32)
                else:
                    out[begin + BLOCK :, :] += added

    needed = jnp.maximum(2 * here - starts[0], 2 * here + 1 - starts[1]) + 1
    for number, reach in enumerate(REACHES):
        below = REACHES[number - 1] if number else 0
        pl.when((needed > below) & (needed <= reach))(functools.partial(work, reach))

    for part, (total, factor) in enumerate(((dk, SCALE), (dv, None))):
        scaled = total[...] if factor is None else total[...] * factor
        at = part * HD
        kept_ref[:, at : at + HD] = scaled[896:1152, :]
        kept_ref[:, 256 + at : 256 + at + HD] = scaled[384:640, :]
        kept_ref[0:128, 512 + at : 512 + at + HD] = jnp.zeros((128, HD), jnp.float32)
        kept_ref[128:256, 512 + at : 512 + at + HD] = scaled[0:128, :]
        sent_ref[:, at : at + HD] = scaled[640:896, :].astype(jnp.bfloat16)
        sent_ref[:, 256 + at : 256 + at + HD] = scaled[128:384, :].astype(jnp.bfloat16)


def attention(doc_blocks, qg, *pieces):
    vmem = pl.BlockSpec(memory_space=pltpu.VMEM)
    window = WINDOW * BLOCK
    return pl.pallas_call(
        attention_kernel,
        out_shape=(
            jax.ShapeDtypeStruct((ROWS, HEADS * HD), jnp.bfloat16),
            jax.ShapeDtypeStruct((ROWS, HEADS * HD), jnp.bfloat16),
            jax.ShapeDtypeStruct((ROWS, 6 * HD), jnp.float32),
            jax.ShapeDtypeStruct((ROWS, 4 * HD), jnp.bfloat16),
        ),
        in_specs=[pl.BlockSpec(memory_space=pltpu.SMEM)] + [vmem] * 6,
        out_specs=(vmem, vmem, vmem, vmem),
        scratch_shapes=[
            pltpu.VMEM((window, HD), jnp.bfloat16),
            pltpu.VMEM((window, HD), jnp.bfloat16),
            pltpu.VMEM((HD, window), jnp.bfloat16),
            pltpu.VMEM((HD, window), jnp.bfloat16),
            pltpu.VMEM((window, HD), jnp.float32),
            pltpu.VMEM((window, HD), jnp.float32),
            pltpu.VMEM((2, REACH * BLOCK, 2 * BLOCK), jnp.float32),
            pltpu.VMEM((2, REACH * BLOCK, HEADS * BLOCK), jnp.bfloat16),
            pltpu.VMEM((2, REACH * BLOCK, HEADS * BLOCK), jnp.bfloat16),
            pltpu.VMEM((2, HEADS * BLOCK, HD), jnp.bfloat16),
            pltpu.VMEM((2, HEADS * BLOCK, HD), jnp.bfloat16),
        ],
        compiler_params=pltpu.CompilerParams(vmem_limit_bytes=40 * 1024 * 1024),
        cost_estimate=pl.CostEstimate(
            flops=3_000_000_000, bytes_accessed=4_000_000, transcendentals=2_100_000
        ),
    )(doc_blocks, qg, *pieces)


def shifted(block, distance):
    devices = range(lax.axis_size("seq"))
    route = [(i - distance, i) for i in devices if i - distance in devices]
    return lax.ppermute(block, "seq", route)


def partners(block):
    return lax.ppermute(block, "seq", [(i, i ^ 1) for i in range(lax.axis_size("seq"))])


def exchanged(chunks):
    received = lax.all_to_all(chunks, "head", split_axis=0, concat_axis=0, tiled=True)
    return received.reshape(-1, chunks.shape[2])


def packing_kernel(queries_ref, grad_out_ref, chunks_ref, held, in_sems, out_sems):
    groups, _, width = chunks_ref.shape
    half = width // 2

    def arriving(part, group):
        source = (queries_ref, grad_out_ref)[part]
        return pltpu.make_async_copy(
            source.at[:, pl.ds(group * half, half)],
            held.at[group, :, pl.ds(part * half, half)],
            in_sems.at[part, group],
        )

    def leaving(group):
        return pltpu.make_async_copy(held.at[group], chunks_ref.at[group], out_sems.at[group])

    for group in range(groups):
        for part in range(2):
            arriving(part, group).start()
    for group in range(groups):
        for part in range(2):
            arriving(part, group).wait()
        leaving(group).start()
    for group in range(groups):
        leaving(group).wait()


def packed(queries, grad_out):
    groups = lax.axis_size("head")
    rows, columns = queries.shape
    chunks = (groups, rows, 2 * columns // groups)
    anywhere = pl.BlockSpec(memory_space=pl.ANY)
    return pl.pallas_call(
        packing_kernel,
        out_shape=jax.ShapeDtypeStruct(chunks, queries.dtype),
        in_specs=[anywhere] * 2,
        out_specs=anywhere,
        scratch_shapes=[
            pltpu.VMEM(chunks, queries.dtype),
            pltpu.SemaphoreType.DMA((2, groups)),
            pltpu.SemaphoreType.DMA((groups,)),
        ],
        cost_estimate=pl.CostEstimate(flops=0, bytes_accessed=2_100_000, transcendentals=0),
    )(queries, grad_out)


def piling_kernel(keys_ref, values_ref, chunks_ref):
    for group in range(chunks_ref.shape[0]):
        for part, source in enumerate((keys_ref, values_ref)):
            chunks_ref[group, :, part * HD : (part + 1) * HD] = source[
                :, group * HD : (group + 1) * HD
            ]


def piled(keys, values):
    groups = lax.axis_size("head")
    vmem = pl.BlockSpec(memory_space=pltpu.VMEM)
    return pl.pallas_call(
        piling_kernel,
        out_shape=jax.ShapeDtypeStruct((groups, keys.shape[0], 2 * HD), keys.dtype),
        in_specs=[vmem] * 2,
        out_specs=vmem,
        cost_estimate=pl.CostEstimate(flops=0, bytes_accessed=260_000, transcendentals=0),
    )(keys, values)


def local(queries, keys, values, grad_out, doc_blocks):
    odd = lax.rem(lax.axis_index("seq"), 2) == 1
    own = exchanged(piled(keys, values))
    chunks, own = lax.optimization_barrier((packed(queries, grad_out), own))
    qg = exchanged(chunks)
    two = shifted(own, 2)
    four = shifted(own, 4)
    their_two = partners(two)
    their_other = partners(jnp.where(odd, four, own))
    attended, grad_queries, kept, sent = attention(
        doc_blocks, qg, own, two, four, their_two, their_other
    )
    swapped = partners(sent).astype(jnp.float32)
    one, three = swapped[:, 0:256], swapped[:, 256:512]
    for_here = kept[:, 0:256] + jnp.where(odd, 0.0, one)
    for_two = (kept[:, 256:512] + jnp.where(odd, one, three)).astype(jnp.bfloat16)
    for_four = (kept[:, 512:768] + jnp.where(odd, three, 0.0)).astype(jnp.bfloat16)
    with_four = lax.optimization_barrier(for_here + shifted(for_four, -4).astype(jnp.float32))
    total = (with_four + shifted(for_two, -2).astype(jnp.float32)).astype(jnp.bfloat16)
    return attended, grad_queries, total[:, 0:128], total[:, 128:256]


def solution(mesh):
    rows = P(("seq", "head"), None)
    return jax.shard_map(
        local,
        mesh=mesh,
        in_specs=(rows, rows, rows, rows, P()),
        out_specs=(P("seq", "head"),) * 4,
        check_vma=False,
    )
```

```python
import functools

import jax
import jax.numpy as jnp
from jax import lax
from jax.experimental import pallas as pl
from jax.experimental.pallas import tpu as pltpu
from jax.sharding import PartitionSpec as P

HD = 128
BLOCK = 128
HEADS = 8
ROWS = 256
SCALE = HD**-0.5
EXP2_SCALE = SCALE * 1.4426950408889634
WINDOW = 9
REACH = 8
JOINED = (2, 3, 4, 5, 6, 7)
PARTED = (4, 8)


def document_start(doc_ref, block):
    end = jnp.int32(0)
    start = jnp.int32(0)
    for doc in range(doc_ref.shape[0]):
        start = jnp.where(end <= block, end, start)
        end = end + doc_ref[doc]
    return start


def attention_kernel(
    doc_ref, qg_ref, own_ref, two_ref, four_ref, their_two_ref, their_other_ref,
    att_ref, gq_ref, kept_ref, sent_ref,
    kw, vw, kt, vt, dk, dv, scores, weights, grads, qs, gs,
):
    here = lax.axis_index("seq")
    parity = lax.rem(here, 2)
    for part, window in enumerate((kw, vw)):
        columns = pl.ds(part * HD, HD)
        window[0:128, :] = four_ref[128:256, columns]
        window[384:640, :] = two_ref[:, columns]
        window[896:1152, :] = own_ref[:, columns]

    @pl.when(parity == 0)
    def _():
        for part, window in enumerate((kw, vw)):
            columns = pl.ds(part * HD, HD)
            window[128:384, :] = their_other_ref[:, columns]
            window[640:896, :] = their_two_ref[:, columns]

    @pl.when(parity == 1)
    def _():
        for part, window in enumerate((kw, vw)):
            columns = pl.ds(part * HD, HD)
            window[128:384, :] = their_two_ref[:, columns]
            window[640:896, :] = their_other_ref[:, columns]

    kt[...] = kw[...].T
    vt[...] = vw[...].T

    starts = [document_start(doc_ref, 2 * here + half) for half in range(2)]
    key_at = lax.broadcasted_iota(jnp.int32, (BLOCK, 2 * BLOCK), 0)
    query_at = lax.rem(lax.broadcasted_iota(jnp.int32, (BLOCK, 2 * BLOCK), 1), BLOCK)
    causal = key_at <= query_at

    def stacked(ref, half, column):
        rows = pl.ds(half * BLOCK, BLOCK)
        return jnp.concatenate(
            [ref[rows, pl.ds(column + i * HD, HD)] for i in range(2)], axis=0
        )

    def over_sublanes(op, array):
        return op(array.reshape(-1, 8, 2 * BLOCK), axis=0)

    class Unit:
        def __init__(self, number, reaches):
            self.pair, self.half = divmod(number, 2)
            self.slot = number % 2
            reach = reaches[self.half]
            self.begin = REACH - reach
            self.column = self.pair * 2 * HD
            self.columns = pl.ds(self.column, 2 * BLOCK)
            self.low = (self.half + REACH - reach) * BLOCK
            self.high = (self.half + REACH) * BLOCK
            self.rows = pl.ds((REACH - reach) * BLOCK, reach * BLOCK)

        def valid(self, w):
            return 2 * here - 7 + self.half + w >= starts[self.half]

        def load(self):
            q2 = stacked(qg_ref, self.half, self.column)
            self.qt = q2.T
            self.gt = stacked(qg_ref, self.half, HEADS * HD + self.column).T
            qs[self.half, self.columns, :] = q2
            self.highest = None

        def score(self, w):
            at = (self.half + w) * BLOCK
            score = jnp.dot(kw[at : at + BLOCK, :], self.qt, preferred_element_type=jnp.float32)
            if w == REACH - 1:
                score = jnp.where(causal, score, -1e30)
            scores[self.slot, w * BLOCK : (w + 1) * BLOCK, :] = score
            top = over_sublanes(jnp.max, score)
            if w < REACH - 1:
                top = jnp.where(self.valid(w), top, -1e30)
            self.highest = top if self.highest is None else jnp.maximum(self.highest, top)

        def level(self):
            self.shift = jnp.max(self.highest, axis=0, keepdims=True) * EXP2_SCALE
            self.total = None

        def weigh(self, w):
            rows = pl.ds(w * BLOCK, BLOCK)
            down = self.shift if w == REACH - 1 else jnp.where(self.valid(w), self.shift, 1e30)
            weight = jnp.exp2(scores[self.slot, rows, :] * EXP2_SCALE - down)
            part = over_sublanes(jnp.sum, weight)
            self.total = part if self.total is None else self.total + part
            weights[self.half, rows, self.columns] = weight.astype(jnp.bfloat16)

        def attend(self):
            inverse = 1.0 / jnp.sum(self.total, axis=0, keepdims=True)
            att_t = (
                jnp.dot(
                    vt[:, self.low : self.high],
                    weights[self.half, self.rows, self.columns],
                    preferred_element_type=jnp.float32,
                )
                * inverse
            ).astype(jnp.bfloat16)
            self.scaled_t = (self.gt.astype(jnp.float32) * inverse).astype(jnp.bfloat16)
            gs[self.half, self.columns, :] = self.scaled_t.T
            self.delta = jnp.sum(
                self.scaled_t.astype(jnp.float32) * att_t.astype(jnp.float32),
                axis=0,
                keepdims=True,
            )
            self.store(att_ref, att_t)

        def grade(self, w):
            at = (self.half + w) * BLOCK
            rows = pl.ds(w * BLOCK, BLOCK)
            grad = jnp.dot(
                vw[at : at + BLOCK, :], self.scaled_t, preferred_element_type=jnp.float32
            )
            grads[self.half, rows, self.columns] = (
                weights[self.half, rows, self.columns].astype(jnp.float32) * (grad - self.delta)
            ).astype(jnp.bfloat16)

        def finish(self):
            gq_t = (
                jnp.dot(
                    kt[:, self.low : self.high],
                    grads[self.half, self.rows, self.columns],
                    preferred_element_type=jnp.float32,
                )
                * SCALE
            ).astype(jnp.bfloat16)
            self.store(gq_ref, gq_t)

        def store(self, ref, turned):
            for i in range(2):
                ref[
                    pl.ds(self.half * BLOCK, BLOCK), pl.ds(self.column + i * HD, HD)
                ] = turned[:, i * BLOCK : (i + 1) * BLOCK].T

    def work(reaches):
        units = [Unit(number, reaches) for number in range(HEADS)]
        for step in range(len(units) + 2):
            first, second, third = (
                units[step - lag] if 0 <= step - lag < len(units) else None for lag in range(3)
            )
            if first:
                first.load()
            if second:
                second.level()
            for w in range(REACH):
                if first and w >= first.begin:
                    first.score(w)
                if second and w >= second.begin:
                    second.weigh(w)
                if third and w >= third.begin:
                    third.grade(w)
            if second:
                second.attend()
            if third:
                third.finish()
        for out, left, right in ((dv, weights, gs), (dk, grads, qs)):
            for half in range(2):
                begin = (REACH - reaches[half]) * BLOCK
                added = jnp.dot(
                    left[half, begin : REACH * BLOCK, :],
                    right[half],
                    preferred_element_type=jnp.float32,
                )
                if half == 0:
                    if begin:
                        out[0:begin, :] = jnp.zeros((begin, HD), jnp.float32)
                    out[begin : REACH * BLOCK, :] = added
                    out[REACH * BLOCK :, :] = jnp.zeros((BLOCK, HD), jnp.float32)
                else:
                    out[begin + BLOCK :, :] += added

    needed = 2 * here - starts[0] + 1
    joined = starts[0] == starts[1]
    for number, reach in enumerate(JOINED):
        below = JOINED[number - 1] if number else 0
        pl.when(joined & (needed > below) & (needed <= reach))(
            functools.partial(work, (reach, reach + 1))
        )
    for number, reach in enumerate(PARTED):
        below = PARTED[number - 1] if number else 0
        pl.when(~joined & (needed > below) & (needed <= reach))(
            functools.partial(work, (reach, 1))
        )

    for part, (total, factor) in enumerate(((dk, SCALE), (dv, None))):
        scaled = total[...] if factor is None else total[...] * factor
        at = part * HD
        kept_ref[:, at : at + HD] = scaled[896:1152, :]
        kept_ref[:, 256 + at : 256 + at + HD] = scaled[384:640, :]
        kept_ref[0:128, 512 + at : 512 + at + HD] = jnp.zeros((128, HD), jnp.float32)
        kept_ref[128:256, 512 + at : 512 + at + HD] = scaled[0:128, :]
        sent_ref[:, at : at + HD] = scaled[640:896, :].astype(jnp.bfloat16)
        sent_ref[:, 256 + at : 256 + at + HD] = scaled[128:384, :].astype(jnp.bfloat16)


def attention(doc_blocks, qg, *pieces):
    vmem = pl.BlockSpec(memory_space=pltpu.VMEM)
    window = WINDOW * BLOCK
    return pl.pallas_call(
        attention_kernel,
        out_shape=(
            jax.ShapeDtypeStruct((ROWS, HEADS * HD), jnp.bfloat16),
            jax.ShapeDtypeStruct((ROWS, HEADS * HD), jnp.bfloat16),
            jax.ShapeDtypeStruct((ROWS, 6 * HD), jnp.float32),
            jax.ShapeDtypeStruct((ROWS, 4 * HD), jnp.bfloat16),
        ),
        in_specs=[pl.BlockSpec(memory_space=pltpu.SMEM)] + [vmem] * 6,
        out_specs=(vmem, vmem, vmem, vmem),
        scratch_shapes=[
            pltpu.VMEM((window, HD), jnp.bfloat16),
            pltpu.VMEM((window, HD), jnp.bfloat16),
            pltpu.VMEM((HD, window), jnp.bfloat16),
            pltpu.VMEM((HD, window), jnp.bfloat16),
            pltpu.VMEM((window, HD), jnp.float32),
            pltpu.VMEM((window, HD), jnp.float32),
            pltpu.VMEM((2, REACH * BLOCK, 2 * BLOCK), jnp.float32),
            pltpu.VMEM((2, REACH * BLOCK, HEADS * BLOCK), jnp.bfloat16),
            pltpu.VMEM((2, REACH * BLOCK, HEADS * BLOCK), jnp.bfloat16),
            pltpu.VMEM((2, HEADS * BLOCK, HD), jnp.bfloat16),
            pltpu.VMEM((2, HEADS * BLOCK, HD), jnp.bfloat16),
        ],
        compiler_params=pltpu.CompilerParams(vmem_limit_bytes=40 * 1024 * 1024),
        cost_estimate=pl.CostEstimate(
            flops=3_000_000_000, bytes_accessed=4_000_000, transcendentals=2_100_000
        ),
    )(doc_blocks, qg, *pieces)


def shifted(block, distance):
    devices = range(lax.axis_size("seq"))
    route = [(i - distance, i) for i in devices if i - distance in devices]
    return lax.ppermute(block, "seq", route)


def partners(block):
    return lax.ppermute(block, "seq", [(i, i ^ 1) for i in range(lax.axis_size("seq"))])


def exchanged(chunks):
    received = lax.all_to_all(chunks, "head", split_axis=0, concat_axis=0, tiled=True)
    return received.reshape(-1, chunks.shape[2])


def packing_kernel(queries_ref, grad_out_ref, chunks_ref, held, in_sems, out_sems):
    groups, _, width = chunks_ref.shape
    half = width // 2

    def arriving(part, group):
        source = (queries_ref, grad_out_ref)[part]
        return pltpu.make_async_copy(
            source.at[:, pl.ds(group * half, half)],
            held.at[group, :, pl.ds(part * half, half)],
            in_sems.at[part, group],
        )

    def leaving(group):
        return pltpu.make_async_copy(held.at[group], chunks_ref.at[group], out_sems.at[group])

    for group in range(groups):
        for part in range(2):
            arriving(part, group).start()
    for group in range(groups):
        for part in range(2):
            arriving(part, group).wait()
        leaving(group).start()
    for group in range(groups):
        leaving(group).wait()


def packed(queries, grad_out):
    groups = lax.axis_size("head")
    rows, columns = queries.shape
    chunks = (groups, rows, 2 * columns // groups)
    anywhere = pl.BlockSpec(memory_space=pl.ANY)
    return pl.pallas_call(
        packing_kernel,
        out_shape=jax.ShapeDtypeStruct(chunks, queries.dtype),
        in_specs=[anywhere] * 2,
        out_specs=anywhere,
        scratch_shapes=[
            pltpu.VMEM(chunks, queries.dtype),
            pltpu.SemaphoreType.DMA((2, groups)),
            pltpu.SemaphoreType.DMA((groups,)),
        ],
        cost_estimate=pl.CostEstimate(flops=0, bytes_accessed=2_100_000, transcendentals=0),
    )(queries, grad_out)


def piling_kernel(keys_ref, values_ref, chunks_ref):
    for group in range(chunks_ref.shape[0]):
        for part, source in enumerate((keys_ref, values_ref)):
            chunks_ref[group, :, part * HD : (part + 1) * HD] = source[
                :, group * HD : (group + 1) * HD
            ]


def piled(keys, values):
    groups = lax.axis_size("head")
    vmem = pl.BlockSpec(memory_space=pltpu.VMEM)
    return pl.pallas_call(
        piling_kernel,
        out_shape=jax.ShapeDtypeStruct((groups, keys.shape[0], 2 * HD), keys.dtype),
        in_specs=[vmem] * 2,
        out_specs=vmem,
        cost_estimate=pl.CostEstimate(flops=0, bytes_accessed=260_000, transcendentals=0),
    )(keys, values)


def local(queries, keys, values, grad_out, doc_blocks):
    odd = lax.rem(lax.axis_index("seq"), 2) == 1
    own = exchanged(piled(keys, values))
    chunks, own = lax.optimization_barrier((packed(queries, grad_out), own))
    qg = exchanged(chunks)
    two = shifted(own, 2)
    four = shifted(own, 4)
    their_two = partners(two)
    their_other = partners(jnp.where(odd, four, own))
    attended, grad_queries, kept, sent = attention(
        doc_blocks, qg, own, two, four, their_two, their_other
    )
    swapped = partners(sent).astype(jnp.float32)
    one, three = swapped[:, 0:256], swapped[:, 256:512]
    for_here = kept[:, 0:256] + jnp.where(odd, 0.0, one)
    for_two = (kept[:, 256:512] + jnp.where(odd, one, three)).astype(jnp.bfloat16)
    for_four = (kept[:, 512:768] + jnp.where(odd, three, 0.0)).astype(jnp.bfloat16)
    with_four = lax.optimization_barrier(for_here + shifted(for_four, -4).astype(jnp.float32))
    total = (with_four + shifted(for_two, -2).astype(jnp.float32)).astype(jnp.bfloat16)
    return attended, grad_queries, total[:, 0:128], total[:, 128:256]


def solution(mesh):
    rows = P(("seq", "head"), None)
    return jax.shard_map(
        local,
        mesh=mesh,
        in_specs=(rows, rows, rows, rows, P()),
        out_specs=(P("seq", "head"),) * 4,
        check_vma=False,
    )
```

```python
import functools

import jax
import jax.numpy as jnp
from jax import lax
from jax.experimental import pallas as pl
from jax.experimental.pallas import tpu as pltpu
from jax.sharding import PartitionSpec as P

HD = 128
BLOCK = 128
HEADS = 8
ROWS = 256
SCALE = HD**-0.5
EXP2_SCALE = SCALE * 1.4426950408889634
WINDOW = 9
REACH = 8
JOINED = (3, 5, 7)
PARTED = (8,)


def document_start(doc_ref, block):
    end = jnp.int32(0)
    start = jnp.int32(0)
    for doc in range(doc_ref.shape[0]):
        start = jnp.where(end <= block, end, start)
        end = end + doc_ref[doc]
    return start


def attention_kernel(
    doc_ref, qg_ref, own_ref, two_ref, four_ref, their_two_ref, their_other_ref,
    att_ref, gq_ref, kept_ref, sent_ref,
    kw, vw, kt, vt, dk, dv, scores, weights, grads, qs, gs,
):
    here = lax.axis_index("seq")
    parity = lax.rem(here, 2)
    for part, window in enumerate((kw, vw)):
        columns = pl.ds(part * HD, HD)
        window[0:128, :] = four_ref[128:256, columns]
        window[384:640, :] = two_ref[:, columns]
        window[896:1152, :] = own_ref[:, columns]

    @pl.when(parity == 0)
    def _():
        for part, window in enumerate((kw, vw)):
            columns = pl.ds(part * HD, HD)
            window[128:384, :] = their_other_ref[:, columns]
            window[640:896, :] = their_two_ref[:, columns]

    @pl.when(parity == 1)
    def _():
        for part, window in enumerate((kw, vw)):
            columns = pl.ds(part * HD, HD)
            window[128:384, :] = their_two_ref[:, columns]
            window[640:896, :] = their_other_ref[:, columns]

    kt[...] = kw[...].T
    vt[...] = vw[...].T

    starts = [document_start(doc_ref, 2 * here + half) for half in range(2)]
    key_at = lax.broadcasted_iota(jnp.int32, (BLOCK, 2 * BLOCK), 0)
    query_at = lax.rem(lax.broadcasted_iota(jnp.int32, (BLOCK, 2 * BLOCK), 1), BLOCK)
    causal = key_at <= query_at

    def stacked(ref, half, column):
        rows = pl.ds(half * BLOCK, BLOCK)
        return jnp.concatenate(
            [ref[rows, pl.ds(column + i * HD, HD)] for i in range(2)], axis=0
        )

    def over_sublanes(op, array):
        return op(array.reshape(-1, 8, 2 * BLOCK), axis=0)

    class Unit:
        def __init__(self, number, reaches):
            self.pair, self.half = divmod(number, 2)
            self.slot = number % 2
            reach = reaches[self.half]
            self.begin = REACH - reach
            self.column = self.pair * 2 * HD
            self.columns = pl.ds(self.column, 2 * BLOCK)
            self.low = (self.half + REACH - reach) * BLOCK
            self.high = (self.half + REACH) * BLOCK
            self.rows = pl.ds((REACH - reach) * BLOCK, reach * BLOCK)

        def valid(self, w):
            return 2 * here - 7 + self.half + w >= starts[self.half]

        def load(self):
            q2 = stacked(qg_ref, self.half, self.column)
            self.qt = q2.T
            self.gt = stacked(qg_ref, self.half, HEADS * HD + self.column).T
            qs[self.half, self.columns, :] = q2
            self.highest = None

        def score(self, w):
            at = (self.half + w) * BLOCK
            score = jnp.dot(kw[at : at + BLOCK, :], self.qt, preferred_element_type=jnp.float32)
            if w == REACH - 1:
                score = jnp.where(causal, score, -1e30)
            scores[self.slot, w * BLOCK : (w + 1) * BLOCK, :] = score
            top = over_sublanes(jnp.max, score)
            if w < REACH - 1:
                top = jnp.where(self.valid(w), top, -1e30)
            self.highest = top if self.highest is None else jnp.maximum(self.highest, top)

        def level(self):
            self.shift = jnp.max(self.highest, axis=0, keepdims=True) * EXP2_SCALE
            self.total = None

        def weigh(self, w):
            rows = pl.ds(w * BLOCK, BLOCK)
            down = self.shift if w == REACH - 1 else jnp.where(self.valid(w), self.shift, 1e30)
            weight = jnp.exp2(scores[self.slot, rows, :] * EXP2_SCALE - down)
            part = over_sublanes(jnp.sum, weight)
            self.total = part if self.total is None else self.total + part
            weights[self.half, rows, self.columns] = weight.astype(jnp.bfloat16)

        def attend(self):
            inverse = 1.0 / jnp.sum(self.total, axis=0, keepdims=True)
            att_t = (
                jnp.dot(
                    vt[:, self.low : self.high],
                    weights[self.half, self.rows, self.columns],
                    preferred_element_type=jnp.float32,
                )
                * inverse
            ).astype(jnp.bfloat16)
            self.scaled_t = (self.gt.astype(jnp.float32) * inverse).astype(jnp.bfloat16)
            gs[self.half, self.columns, :] = self.scaled_t.T
            self.delta = jnp.sum(
                self.scaled_t.astype(jnp.float32) * att_t.astype(jnp.float32),
                axis=0,
                keepdims=True,
            )
            self.store(att_ref, att_t)

        def grade(self, w):
            at = (self.half + w) * BLOCK
            rows = pl.ds(w * BLOCK, BLOCK)
            grad = jnp.dot(
                vw[at : at + BLOCK, :], self.scaled_t, preferred_element_type=jnp.float32
            )
            grads[self.half, rows, self.columns] = (
                weights[self.half, rows, self.columns].astype(jnp.float32) * (grad - self.delta)
            ).astype(jnp.bfloat16)

        def finish(self):
            gq_t = (
                jnp.dot(
                    kt[:, self.low : self.high],
                    grads[self.half, self.rows, self.columns],
                    preferred_element_type=jnp.float32,
                )
                * SCALE
            ).astype(jnp.bfloat16)
            self.store(gq_ref, gq_t)

        def store(self, ref, turned):
            for i in range(2):
                ref[
                    pl.ds(self.half * BLOCK, BLOCK), pl.ds(self.column + i * HD, HD)
                ] = turned[:, i * BLOCK : (i + 1) * BLOCK].T

    def work(reaches):
        units = [Unit(number, reaches) for number in range(HEADS)]
        for step in range(len(units) + 2):
            first, second, third = (
                units[step - lag] if 0 <= step - lag < len(units) else None for lag in range(3)
            )
            if first:
                first.load()
            if second:
                second.level()
            for w in range(REACH):
                if first and w >= first.begin:
                    first.score(w)
                if second and w >= second.begin:
                    second.weigh(w)
                if third and w >= third.begin:
                    third.grade(w)
            if second:
                second.attend()
            if third:
                third.finish()
        for out, left, right in ((dv, weights, gs), (dk, grads, qs)):
            for half in range(2):
                begin = (REACH - reaches[half]) * BLOCK
                added = jnp.dot(
                    left[half, begin : REACH * BLOCK, :],
                    right[half],
                    preferred_element_type=jnp.float32,
                )
                if half == 0:
                    if begin:
                        out[0:begin, :] = jnp.zeros((begin, HD), jnp.float32)
                    out[begin : REACH * BLOCK, :] = added
                    out[REACH * BLOCK :, :] = jnp.zeros((BLOCK, HD), jnp.float32)
                else:
                    out[begin + BLOCK :, :] += added

    needed = 2 * here - starts[0] + 1
    joined = starts[0] == starts[1]
    for number, reach in enumerate(JOINED):
        below = JOINED[number - 1] if number else 0
        pl.when(joined & (needed > below) & (needed <= reach))(
            functools.partial(work, (reach, reach + 1))
        )
    for number, reach in enumerate(PARTED):
        below = PARTED[number - 1] if number else 0
        pl.when(~joined & (needed > below) & (needed <= reach))(
            functools.partial(work, (reach, 1))
        )

    for part, (total, factor) in enumerate(((dk, SCALE), (dv, None))):
        scaled = total[...] if factor is None else total[...] * factor
        at = part * HD
        kept_ref[:, at : at + HD] = scaled[896:1152, :]
        kept_ref[:, 256 + at : 256 + at + HD] = scaled[384:640, :]
        kept_ref[0:128, 512 + at : 512 + at + HD] = jnp.zeros((128, HD), jnp.float32)
        kept_ref[128:256, 512 + at : 512 + at + HD] = scaled[0:128, :]
        sent_ref[:, at : at + HD] = scaled[640:896, :].astype(jnp.bfloat16)
        sent_ref[:, 256 + at : 256 + at + HD] = scaled[128:384, :].astype(jnp.bfloat16)


def attention(doc_blocks, qg, *pieces):
    vmem = pl.BlockSpec(memory_space=pltpu.VMEM)
    window = WINDOW * BLOCK
    return pl.pallas_call(
        attention_kernel,
        out_shape=(
            jax.ShapeDtypeStruct((ROWS, HEADS * HD), jnp.bfloat16),
            jax.ShapeDtypeStruct((ROWS, HEADS * HD), jnp.bfloat16),
            jax.ShapeDtypeStruct((ROWS, 6 * HD), jnp.float32),
            jax.ShapeDtypeStruct((ROWS, 4 * HD), jnp.bfloat16),
        ),
        in_specs=[pl.BlockSpec(memory_space=pltpu.SMEM)] + [vmem] * 6,
        out_specs=(vmem, vmem, vmem, vmem),
        scratch_shapes=[
            pltpu.VMEM((window, HD), jnp.bfloat16),
            pltpu.VMEM((window, HD), jnp.bfloat16),
            pltpu.VMEM((HD, window), jnp.bfloat16),
            pltpu.VMEM((HD, window), jnp.bfloat16),
            pltpu.VMEM((window, HD), jnp.float32),
            pltpu.VMEM((window, HD), jnp.float32),
            pltpu.VMEM((2, REACH * BLOCK, 2 * BLOCK), jnp.float32),
            pltpu.VMEM((2, REACH * BLOCK, HEADS * BLOCK), jnp.bfloat16),
            pltpu.VMEM((2, REACH * BLOCK, HEADS * BLOCK), jnp.bfloat16),
            pltpu.VMEM((2, HEADS * BLOCK, HD), jnp.bfloat16),
            pltpu.VMEM((2, HEADS * BLOCK, HD), jnp.bfloat16),
        ],
        compiler_params=pltpu.CompilerParams(vmem_limit_bytes=40 * 1024 * 1024),
        cost_estimate=pl.CostEstimate(
            flops=3_000_000_000, bytes_accessed=4_000_000, transcendentals=2_100_000
        ),
    )(doc_blocks, qg, *pieces)


def shifted(block, distance):
    devices = range(lax.axis_size("seq"))
    route = [(i - distance, i) for i in devices if i - distance in devices]
    return lax.ppermute(block, "seq", route)


def partners(block):
    return lax.ppermute(block, "seq", [(i, i ^ 1) for i in range(lax.axis_size("seq"))])


def exchanged(chunks):
    received = lax.all_to_all(chunks, "head", split_axis=0, concat_axis=0, tiled=True)
    return received.reshape(-1, chunks.shape[2])


def packing_kernel(queries_ref, grad_out_ref, chunks_ref, held, in_sems, out_sems):
    groups, _, width = chunks_ref.shape
    half = width // 2

    def arriving(part, group):
        source = (queries_ref, grad_out_ref)[part]
        return pltpu.make_async_copy(
            source.at[:, pl.ds(group * half, half)],
            held.at[group, :, pl.ds(part * half, half)],
            in_sems.at[part, group],
        )

    def leaving(group):
        return pltpu.make_async_copy(held.at[group], chunks_ref.at[group], out_sems.at[group])

    for group in range(groups):
        for part in range(2):
            arriving(part, group).start()
    for group in range(groups):
        for part in range(2):
            arriving(part, group).wait()
        leaving(group).start()
    for group in range(groups):
        leaving(group).wait()


def packed(queries, grad_out):
    groups = lax.axis_size("head")
    rows, columns = queries.shape
    chunks = (groups, rows, 2 * columns // groups)
    anywhere = pl.BlockSpec(memory_space=pl.ANY)
    return pl.pallas_call(
        packing_kernel,
        out_shape=jax.ShapeDtypeStruct(chunks, queries.dtype),
        in_specs=[anywhere] * 2,
        out_specs=anywhere,
        scratch_shapes=[
            pltpu.VMEM(chunks, queries.dtype),
            pltpu.SemaphoreType.DMA((2, groups)),
            pltpu.SemaphoreType.DMA((groups,)),
        ],
        cost_estimate=pl.CostEstimate(flops=0, bytes_accessed=2_100_000, transcendentals=0),
    )(queries, grad_out)


def piling_kernel(keys_ref, values_ref, chunks_ref):
    for group in range(chunks_ref.shape[0]):
        for part, source in enumerate((keys_ref, values_ref)):
            chunks_ref[group, :, part * HD : (part + 1) * HD] = source[
                :, group * HD : (group + 1) * HD
            ]


def piled(keys, values):
    groups = lax.axis_size("head")
    vmem = pl.BlockSpec(memory_space=pltpu.VMEM)
    return pl.pallas_call(
        piling_kernel,
        out_shape=jax.ShapeDtypeStruct((groups, keys.shape[0], 2 * HD), keys.dtype),
        in_specs=[vmem] * 2,
        out_specs=vmem,
        cost_estimate=pl.CostEstimate(flops=0, bytes_accessed=260_000, transcendentals=0),
    )(keys, values)


def local(queries, keys, values, grad_out, doc_blocks):
    odd = lax.rem(lax.axis_index("seq"), 2) == 1
    own = exchanged(piled(keys, values))
    chunks, own = lax.optimization_barrier((packed(queries, grad_out), own))
    qg = exchanged(chunks)
    two = shifted(own, 2)
    four = shifted(own, 4)
    their_two = partners(two)
    their_other = partners(jnp.where(odd, four, own))
    attended, grad_queries, kept, sent = attention(
        doc_blocks, qg, own, two, four, their_two, their_other
    )
    swapped = partners(sent).astype(jnp.float32)
    one, three = swapped[:, 0:256], swapped[:, 256:512]
    for_here = kept[:, 0:256] + jnp.where(odd, 0.0, one)
    for_two = (kept[:, 256:512] + jnp.where(odd, one, three)).astype(jnp.bfloat16)
    for_four = (kept[:, 512:768] + jnp.where(odd, three, 0.0)).astype(jnp.bfloat16)
    with_four = lax.optimization_barrier(for_here + shifted(for_four, -4).astype(jnp.float32))
    total = (with_four + shifted(for_two, -2).astype(jnp.float32)).astype(jnp.bfloat16)
    return attended, grad_queries, total[:, 0:128], total[:, 128:256]


def solution(mesh):
    rows = P(("seq", "head"), None)
    return jax.shard_map(
        local,
        mesh=mesh,
        in_specs=(rows, rows, rows, rows, P()),
        out_specs=(P("seq", "head"),) * 4,
        check_vma=False,
    )
```

```python
import functools

import jax
import jax.numpy as jnp
from jax import lax
from jax.experimental import pallas as pl
from jax.experimental.pallas import tpu as pltpu
from jax.sharding import PartitionSpec as P

HD = 128
BLOCK = 128
HEADS = 8
ROWS = 256
SCALE = HD**-0.5
EXP2_SCALE = SCALE * 1.4426950408889634
WINDOW = 9
REACH = 8
JOINED = (2, 4, 7)
PARTED = (8,)


def document_start(doc_ref, block):
    end = jnp.int32(0)
    start = jnp.int32(0)
    for doc in range(doc_ref.shape[0]):
        start = jnp.where(end <= block, end, start)
        end = end + doc_ref[doc]
    return start


def attention_kernel(
    doc_ref, qg_ref, own_ref, two_ref, four_ref, their_two_ref, their_other_ref,
    att_ref, gq_ref, kept_ref, sent_ref,
    kw, vw, kt, vt, dk, dv, scores, weights, grads, qs, gs,
):
    here = lax.axis_index("seq")
    parity = lax.rem(here, 2)
    for part, window in enumerate((kw, vw)):
        columns = pl.ds(part * HD, HD)
        window[0:128, :] = four_ref[128:256, columns]
        window[384:640, :] = two_ref[:, columns]
        window[896:1152, :] = own_ref[:, columns]

    @pl.when(parity == 0)
    def _():
        for part, window in enumerate((kw, vw)):
            columns = pl.ds(part * HD, HD)
            window[128:384, :] = their_other_ref[:, columns]
            window[640:896, :] = their_two_ref[:, columns]

    @pl.when(parity == 1)
    def _():
        for part, window in enumerate((kw, vw)):
            columns = pl.ds(part * HD, HD)
            window[128:384, :] = their_two_ref[:, columns]
            window[640:896, :] = their_other_ref[:, columns]

    kt[...] = kw[...].T
    vt[...] = vw[...].T

    starts = [document_start(doc_ref, 2 * here + half) for half in range(2)]
    key_at = lax.broadcasted_iota(jnp.int32, (BLOCK, 2 * BLOCK), 0)
    query_at = lax.rem(lax.broadcasted_iota(jnp.int32, (BLOCK, 2 * BLOCK), 1), BLOCK)
    causal = key_at <= query_at

    def stacked(ref, half, column):
        rows = pl.ds(half * BLOCK, BLOCK)
        return jnp.concatenate(
            [ref[rows, pl.ds(column + i * HD, HD)] for i in range(2)], axis=0
        )

    def over_sublanes(op, array):
        return op(array.reshape(-1, 8, 2 * BLOCK), axis=0)

    class Unit:
        def __init__(self, number, reaches):
            self.pair, self.half = divmod(number, 2)
            self.slot = number % 2
            reach = reaches[self.half]
            self.begin = REACH - reach
            self.column = self.pair * 2 * HD
            self.columns = pl.ds(self.column, 2 * BLOCK)
            self.low = (self.half + REACH - reach) * BLOCK
            self.high = (self.half + REACH) * BLOCK
            self.rows = pl.ds((REACH - reach) * BLOCK, reach * BLOCK)

        def valid(self, w):
            return 2 * here - 7 + self.half + w >= starts[self.half]

        def load(self):
            q2 = stacked(qg_ref, self.half, self.column)
            self.qt = q2.T
            self.gt = stacked(qg_ref, self.half, HEADS * HD + self.column).T
            qs[self.half, self.columns, :] = q2
            self.highest = None

        def score(self, w):
            at = (self.half + w) * BLOCK
            score = jnp.dot(kw[at : at + BLOCK, :], self.qt, preferred_element_type=jnp.float32)
            if w == REACH - 1:
                score = jnp.where(causal, score, -1e30)
            scores[self.slot, w * BLOCK : (w + 1) * BLOCK, :] = score
            top = over_sublanes(jnp.max, score)
            if w < REACH - 1:
                top = jnp.where(self.valid(w), top, -1e30)
            self.highest = top if self.highest is None else jnp.maximum(self.highest, top)

        def level(self):
            self.shift = jnp.max(self.highest, axis=0, keepdims=True) * EXP2_SCALE
            self.total = None

        def weigh(self, w):
            rows = pl.ds(w * BLOCK, BLOCK)
            down = self.shift if w == REACH - 1 else jnp.where(self.valid(w), self.shift, 1e30)
            weight = jnp.exp2(scores[self.slot, rows, :] * EXP2_SCALE - down)
            part = over_sublanes(jnp.sum, weight)
            self.total = part if self.total is None else self.total + part
            weights[self.half, rows, self.columns] = weight.astype(jnp.bfloat16)

        def attend(self):
            inverse = 1.0 / jnp.sum(self.total, axis=0, keepdims=True)
            att_t = (
                jnp.dot(
                    vt[:, self.low : self.high],
                    weights[self.half, self.rows, self.columns],
                    preferred_element_type=jnp.float32,
                )
                * inverse
            ).astype(jnp.bfloat16)
            self.scaled_t = (self.gt.astype(jnp.float32) * inverse).astype(jnp.bfloat16)
            gs[self.half, self.columns, :] = self.scaled_t.T
            self.delta = jnp.sum(
                self.scaled_t.astype(jnp.float32) * att_t.astype(jnp.float32),
                axis=0,
                keepdims=True,
            )
            self.store(att_ref, att_t)

        def grade(self, w):
            at = (self.half + w) * BLOCK
            rows = pl.ds(w * BLOCK, BLOCK)
            grad = jnp.dot(
                vw[at : at + BLOCK, :], self.scaled_t, preferred_element_type=jnp.float32
            )
            grads[self.half, rows, self.columns] = (
                weights[self.half, rows, self.columns].astype(jnp.float32) * (grad - self.delta)
            ).astype(jnp.bfloat16)

        def finish(self):
            gq_t = (
                jnp.dot(
                    kt[:, self.low : self.high],
                    grads[self.half, self.rows, self.columns],
                    preferred_element_type=jnp.float32,
                )
                * SCALE
            ).astype(jnp.bfloat16)
            self.store(gq_ref, gq_t)

        def store(self, ref, turned):
            for i in range(2):
                ref[
                    pl.ds(self.half * BLOCK, BLOCK), pl.ds(self.column + i * HD, HD)
                ] = turned[:, i * BLOCK : (i + 1) * BLOCK].T

    def work(reaches):
        units = [Unit(number, reaches) for number in range(HEADS)]
        for step in range(len(units) + 2):
            first, second, third = (
                units[step - lag] if 0 <= step - lag < len(units) else None for lag in range(3)
            )
            if first:
                first.load()
            if second:
                second.level()
            for w in range(REACH):
                if first and w >= first.begin:
                    first.score(w)
                if second and w >= second.begin:
                    second.weigh(w)
                if third and w >= third.begin:
                    third.grade(w)
            if second:
                second.attend()
            if third:
                third.finish()
        for out, left, right in ((dv, weights, gs), (dk, grads, qs)):
            for half in range(2):
                begin = (REACH - reaches[half]) * BLOCK
                added = jnp.dot(
                    left[half, begin : REACH * BLOCK, :],
                    right[half],
                    preferred_element_type=jnp.float32,
                )
                if half == 0:
                    if begin:
                        out[0:begin, :] = jnp.zeros((begin, HD), jnp.float32)
                    out[begin : REACH * BLOCK, :] = added
                    out[REACH * BLOCK :, :] = jnp.zeros((BLOCK, HD), jnp.float32)
                else:
                    out[begin + BLOCK :, :] += added

    needed = 2 * here - starts[0] + 1
    joined = starts[0] == starts[1]
    for number, reach in enumerate(JOINED):
        below = JOINED[number - 1] if number else 0
        pl.when(joined & (needed > below) & (needed <= reach))(
            functools.partial(work, (reach, reach + 1))
        )
    for number, reach in enumerate(PARTED):
        below = PARTED[number - 1] if number else 0
        pl.when(~joined & (needed > below) & (needed <= reach))(
            functools.partial(work, (reach, 1))
        )

    for part, (total, factor) in enumerate(((dk, SCALE), (dv, None))):
        scaled = total[...] if factor is None else total[...] * factor
        at = part * HD
        kept_ref[:, at : at + HD] = scaled[896:1152, :]
        kept_ref[:, 256 + at : 256 + at + HD] = scaled[384:640, :]
        kept_ref[0:128, 512 + at : 512 + at + HD] = jnp.zeros((128, HD), jnp.float32)
        kept_ref[128:256, 512 + at : 512 + at + HD] = scaled[0:128, :]
        sent_ref[:, at : at + HD] = scaled[640:896, :].astype(jnp.bfloat16)
        sent_ref[:, 256 + at : 256 + at + HD] = scaled[128:384, :].astype(jnp.bfloat16)


def attention(doc_blocks, qg, *pieces):
    vmem = pl.BlockSpec(memory_space=pltpu.VMEM)
    window = WINDOW * BLOCK
    return pl.pallas_call(
        attention_kernel,
        out_shape=(
            jax.ShapeDtypeStruct((ROWS, HEADS * HD), jnp.bfloat16),
            jax.ShapeDtypeStruct((ROWS, HEADS * HD), jnp.bfloat16),
            jax.ShapeDtypeStruct((ROWS, 6 * HD), jnp.float32),
            jax.ShapeDtypeStruct((ROWS, 4 * HD), jnp.bfloat16),
        ),
        in_specs=[pl.BlockSpec(memory_space=pltpu.SMEM)] + [vmem] * 6,
        out_specs=(vmem, vmem, vmem, vmem),
        scratch_shapes=[
            pltpu.VMEM((window, HD), jnp.bfloat16),
            pltpu.VMEM((window, HD), jnp.bfloat16),
            pltpu.VMEM((HD, window), jnp.bfloat16),
            pltpu.VMEM((HD, window), jnp.bfloat16),
            pltpu.VMEM((window, HD), jnp.float32),
            pltpu.VMEM((window, HD), jnp.float32),
            pltpu.VMEM((2, REACH * BLOCK, 2 * BLOCK), jnp.float32),
            pltpu.VMEM((2, REACH * BLOCK, HEADS * BLOCK), jnp.bfloat16),
            pltpu.VMEM((2, REACH * BLOCK, HEADS * BLOCK), jnp.bfloat16),
            pltpu.VMEM((2, HEADS * BLOCK, HD), jnp.bfloat16),
            pltpu.VMEM((2, HEADS * BLOCK, HD), jnp.bfloat16),
        ],
        compiler_params=pltpu.CompilerParams(vmem_limit_bytes=40 * 1024 * 1024),
        cost_estimate=pl.CostEstimate(
            flops=3_000_000_000, bytes_accessed=4_000_000, transcendentals=2_100_000
        ),
    )(doc_blocks, qg, *pieces)


def shifted(block, distance):
    devices = range(lax.axis_size("seq"))
    route = [(i - distance, i) for i in devices if i - distance in devices]
    return lax.ppermute(block, "seq", route)


def partners(block):
    return lax.ppermute(block, "seq", [(i, i ^ 1) for i in range(lax.axis_size("seq"))])


def exchanged(chunks):
    received = lax.all_to_all(chunks, "head", split_axis=0, concat_axis=0, tiled=True)
    return received.reshape(-1, chunks.shape[2])


def packing_kernel(queries_ref, grad_out_ref, chunks_ref, held, in_sems, out_sems):
    groups, _, width = chunks_ref.shape
    half = width // 2

    def arriving(part, group):
        source = (queries_ref, grad_out_ref)[part]
        return pltpu.make_async_copy(
            source.at[:, pl.ds(group * half, half)],
            held.at[group, :, pl.ds(part * half, half)],
            in_sems.at[part, group],
        )

    def leaving(group):
        return pltpu.make_async_copy(held.at[group], chunks_ref.at[group], out_sems.at[group])

    for group in range(groups):
        for part in range(2):
            arriving(part, group).start()
    for group in range(groups):
        for part in range(2):
            arriving(part, group).wait()
        leaving(group).start()
    for group in range(groups):
        leaving(group).wait()


def packed(queries, grad_out):
    groups = lax.axis_size("head")
    rows, columns = queries.shape
    chunks = (groups, rows, 2 * columns // groups)
    anywhere = pl.BlockSpec(memory_space=pl.ANY)
    return pl.pallas_call(
        packing_kernel,
        out_shape=jax.ShapeDtypeStruct(chunks, queries.dtype),
        in_specs=[anywhere] * 2,
        out_specs=anywhere,
        scratch_shapes=[
            pltpu.VMEM(chunks, queries.dtype),
            pltpu.SemaphoreType.DMA((2, groups)),
            pltpu.SemaphoreType.DMA((groups,)),
        ],
        cost_estimate=pl.CostEstimate(flops=0, bytes_accessed=2_100_000, transcendentals=0),
    )(queries, grad_out)


def piling_kernel(keys_ref, values_ref, chunks_ref):
    for group in range(chunks_ref.shape[0]):
        for part, source in enumerate((keys_ref, values_ref)):
            chunks_ref[group, :, part * HD : (part + 1) * HD] = source[
                :, group * HD : (group + 1) * HD
            ]


def piled(keys, values):
    groups = lax.axis_size("head")
    vmem = pl.BlockSpec(memory_space=pltpu.VMEM)
    return pl.pallas_call(
        piling_kernel,
        out_shape=jax.ShapeDtypeStruct((groups, keys.shape[0], 2 * HD), keys.dtype),
        in_specs=[vmem] * 2,
        out_specs=vmem,
        cost_estimate=pl.CostEstimate(flops=0, bytes_accessed=260_000, transcendentals=0),
    )(keys, values)


def local(queries, keys, values, grad_out, doc_blocks):
    odd = lax.rem(lax.axis_index("seq"), 2) == 1
    own = exchanged(piled(keys, values))
    chunks, own = lax.optimization_barrier((packed(queries, grad_out), own))
    qg = exchanged(chunks)
    two = shifted(own, 2)
    four = shifted(own, 4)
    their_two = partners(two)
    their_other = partners(jnp.where(odd, four, own))
    attended, grad_queries, kept, sent = attention(
        doc_blocks, qg, own, two, four, their_two, their_other
    )
    swapped = partners(sent).astype(jnp.float32)
    one, three = swapped[:, 0:256], swapped[:, 256:512]
    for_here = kept[:, 0:256] + jnp.where(odd, 0.0, one)
    for_two = (kept[:, 256:512] + jnp.where(odd, one, three)).astype(jnp.bfloat16)
    for_four = (kept[:, 512:768] + jnp.where(odd, three, 0.0)).astype(jnp.bfloat16)
    with_four = lax.optimization_barrier(for_here + shifted(for_four, -4).astype(jnp.float32))
    total = (with_four + shifted(for_two, -2).astype(jnp.float32)).astype(jnp.bfloat16)
    return attended, grad_queries, total[:, 0:128], total[:, 128:256]


def solution(mesh):
    rows = P(("seq", "head"), None)
    return jax.shard_map(
        local,
        mesh=mesh,
        in_specs=(rows, rows, rows, rows, P()),
        out_specs=(P("seq", "head"),) * 4,
        check_vma=False,
    )
```
